256 devices in a mesh: region: 32 (over y, x, z_lo), wshard: 8 (over z_hi, core).
Axes of the slice: x: 4, y: 4, z: 8 (z_hi: 4, z_lo: 2; z = z_hi * 2 + z_lo), core: 2. Of those that a mesh axis runs over, the one named last changes fastest.
Arguments:
- queries: bfloat16 [16384, 1024], P('region', 'wshard'), may hold values from -9 to 9
- mold: bfloat16 [65536, 1024], P('region', 'wshard'), may hold values from -9 to 9
- q_weight: bfloat16 [1024, 1024], P(None, 'wshard'), as said below
- k_weight: bfloat16 [1024, 256], replicated, as said below
- v_weight: bfloat16 [1024, 256], replicated, as said below
- o_weight: bfloat16 [1024, 1024], P('wshard'), may hold values from -0.75 to 0.75
- block_lists: int32 [128, 16], P('region'), may hold values from 0 to 511, as said below
- live_counts: int32 [32], P('region'), may hold values from 1 to 4
Outputs:
- mixed: bfloat16 [16384, 1024], P('region', 'wshard')
The draws below stay inside these ranges and needn't reach their ends.
Inputs may be any that keep to these rules, and one draw needn't show every extreme that they name: `block_lists`: an entry of row b names a mold block of the query block's region r = b // 4 or of region r - 1 or r + 1; entries of one row may repeat. `q_weight`: entries lie within 6 / sqrt(1024) of zero. `k_weight`: entries lie within 6 / sqrt(1024) of zero. `v_weight`: entries lie within 6 / sqrt(1024) of zero.
All inputs are finite; a program needn't handle non-finite values.
Results may differ from the reference program's by a relative error of at most 0.022.
Values may be sent and summed in bfloat16 or wider, within the bound.
A program may use at most 64 MiB of HBM per device.

```python
import jax
import jax.numpy as jnp
from jax import lax

MODEL_WIDTH = 1024
QUERY_HEADS = 16
KEY_VALUE_HEADS = 4
HEAD_SIZE = 64
BLOCK_TOKENS = 128
L = 16
REGION_QBLOCKS = 4
KB_DEV = 16
REGION_COUNT = 32
NQB = 128
MOLD_BLOCKS = 512
NQ = 16384
NK = 65536


def dense_weight(key, columns):
    unscaled_values = jax.random.normal(key, (MODEL_WIDTH, columns), dtype=jnp.float32)
    return jnp.clip(unscaled_values, -6.0, 6.0) * MODEL_WIDTH ** (-0.5)


def draw_queries(key, part):
    key = jax.random.fold_in(key, 21)
    value_rows = jnp.clip(jax.random.normal(key, (NQ, MODEL_WIDTH), dtype=jnp.float32) * 1.5, -9.0, 9.0)
    return value_rows.astype(jnp.bfloat16)


def draw_mold(key, part):
    key = jax.random.fold_in(key, 22)
    value_rows = jnp.clip(jax.random.normal(key, (NK, MODEL_WIDTH), dtype=jnp.float32) * 1.5, -9.0, 9.0)
    return value_rows.astype(jnp.bfloat16)


def draw_q_weight(key, part):
    key = jax.random.fold_in(key, 23)
    value_rows = dense_weight(key, QUERY_HEADS * HEAD_SIZE)
    return value_rows.astype(jnp.bfloat16)


def draw_k_weight(key, part):
    key = jax.random.fold_in(key, 24)
    value_rows = dense_weight(key, KEY_VALUE_HEADS * HEAD_SIZE)
    return value_rows.astype(jnp.bfloat16)


def draw_v_weight(key, part):
    key = jax.random.fold_in(key, 25)
    value_rows = dense_weight(key, KEY_VALUE_HEADS * HEAD_SIZE)
    return value_rows.astype(jnp.bfloat16)


def draw_block_lists(key, part):
    key = jax.random.fold_in(key, 11)
    regions = jnp.arange(NQB, dtype=jnp.int32) // REGION_QBLOCKS
    lowest = jnp.maximum(regions - 1, 0) * KB_DEV
    highest = jnp.minimum(regions + 2, REGION_COUNT) * KB_DEV
    raw_bits = jax.random.randint(key, (NQB, L), 0, 1 << 20, dtype=jnp.int32)
    picks = lowest[:, None] + raw_bits % (highest - lowest)[:, None]
    lower_pick = jnp.maximum(regions - 1, 0) * KB_DEV + raw_bits[:, 0] % KB_DEV
    upper_pick = jnp.minimum(regions + 1, REGION_COUNT - 1) * KB_DEV + raw_bits[:, 1] % KB_DEV
    picks = picks.at[:, 0].set(lower_pick)
    picks = picks.at[:, 1].set(upper_pick)
    picks = picks.at[0, 0].set(0)
    picks = picks.at[NQB - 1, 0].set(MOLD_BLOCKS - 1)
    return picks.astype(jnp.int32)


def draw_live_counts(key, part):
    key = jax.random.fold_in(key, 12)
    counts = jax.random.randint(key, (REGION_COUNT,), 1, REGION_QBLOCKS + 1, dtype=jnp.int32)
    second = jax.random.fold_in(key, 1)
    spot = jax.random.randint(second, (), 0, REGION_COUNT, dtype=jnp.int32)
    counts = counts.at[spot].set(REGION_QBLOCKS)
    counts = counts.at[(spot + 1) % REGION_COUNT].set(1)
    return counts.astype(jnp.int32)


def block_scale(key, extent, shards, low, top_value):
    level, own = 1.0, jax.random.fold_in(key, 6)
    for axis_at, blocks in shards:
        heights = jnp.exp(jax.random.uniform(jax.random.fold_in(own, axis_at), (blocks,), jnp.float32, low / len(shards), top_value / len(shards)))
        level = level * jnp.repeat(heights, extent[axis_at] // blocks).reshape([-1 if axis == axis_at else 1 for axis in range(len(extent))])
    return level


def gaussian(rng, dims, scale, most, cuts=(), held_as=jnp.bfloat16):
    gain = block_scale(rng, dims, cuts, -0.22, 0.18) if cuts else 1.0
    entries = jax.random.normal(rng, dims, jnp.float32) * scale * gain
    return jnp.minimum(jnp.maximum(entries, -most), most).astype(held_as)


def setup_inputs(seed: int = 0) -> dict:
    key_of = jax.random.split(jax.random.key(seed), 9)
    return {
        "queries": draw_queries(jax.random.fold_in(key_of[8], 71), 0),
        "mold": draw_mold(jax.random.fold_in(key_of[8], 71), 0),
        "q_weight": draw_q_weight(jax.random.fold_in(key_of[8], 71), 0),
        "k_weight": draw_k_weight(jax.random.fold_in(key_of[8], 71), 0),
        "v_weight": draw_v_weight(jax.random.fold_in(key_of[8], 71), 0),
        "o_weight": gaussian(key_of[5], (QUERY_HEADS * HEAD_SIZE, MODEL_WIDTH), HEAD_SIZE ** -0.5, 0.75, ((0, 8),)),
        "block_lists": draw_block_lists(jax.random.fold_in(key_of[8], 71), 0),
        "live_counts": draw_live_counts(jax.random.fold_in(key_of[8], 71), 0),
    }


def attend_blocks(query_blocks, key_blocks, value_blocks, lists):
    count_q, rows, kv_heads, query_group, width = query_blocks.shape
    listed = lists.shape[1]
    scores = jnp.einsum('bqhge,blshe->bhgqls', query_blocks.astype(jnp.float32), key_blocks.astype(jnp.float32)) * (width ** -0.5)
    same_block = lists[:, :, None] == lists[:, None, :]
    earlier = jnp.tril(jnp.ones((listed, listed), dtype=bool), -1)
    repeated_heads = jnp.any(same_block & earlier[None], axis=2)
    scores = jnp.where(repeated_heads[:, None, None, None, :, None], -1e30, scores)
    scores = scores.reshape(count_q, kv_heads, query_group, rows, listed * rows)
    top = jnp.max(scores, axis=-1, keepdims=True)
    expo = jnp.exp(scores - top)
    probs = (expo / jnp.sum(expo, axis=-1, keepdims=True)).astype(jnp.bfloat16)
    value_rows = value_blocks.reshape(count_q, listed * rows, kv_heads, width)
    mixed_heads = jnp.einsum('bhgqk,bkhe->bqhge', probs.astype(jnp.float32), value_rows.astype(jnp.float32))
    return mixed_heads.reshape(count_q, rows, kv_heads * query_group * width).astype(jnp.bfloat16)


def reference(queries, mold, q_weight, k_weight, v_weight, o_weight, block_lists, live_counts):
    query_group = QUERY_HEADS // KEY_VALUE_HEADS
    every_query = jnp.dot(queries, q_weight, preferred_element_type=jnp.float32).astype(jnp.bfloat16)
    every_key = jnp.dot(mold, k_weight, preferred_element_type=jnp.float32).astype(jnp.bfloat16)
    every_value = jnp.dot(mold, v_weight, preferred_element_type=jnp.float32).astype(jnp.bfloat16)
    key_block_rows = every_key.reshape(MOLD_BLOCKS, BLOCK_TOKENS, KEY_VALUE_HEADS, HEAD_SIZE)
    value_block_rows = every_value.reshape(MOLD_BLOCKS, BLOCK_TOKENS, KEY_VALUE_HEADS, HEAD_SIZE)
    query_by_region = every_query.reshape(REGION_COUNT, REGION_QBLOCKS, BLOCK_TOKENS, KEY_VALUE_HEADS, query_group, HEAD_SIZE)
    l_regions = block_lists.reshape(REGION_COUNT, REGION_QBLOCKS, L)

    def one_region(inputs):
        q_region, lists = inputs
        return attend_blocks(q_region, key_block_rows[lists], value_block_rows[lists], lists)

    attn = lax.map(one_region, (query_by_region, l_regions))
    live_rows = jnp.arange(REGION_QBLOCKS, dtype=jnp.int32)[None, :] < live_counts[:, None]
    attn = jnp.where(live_rows[:, :, None, None], attn, jnp.zeros_like(attn))
    attn = attn.reshape(NQ, QUERY_HEADS * HEAD_SIZE)
    return jnp.dot(attn, o_weight, preferred_element_type=jnp.float32).astype(jnp.bfloat16)
```

```python
import functools

import jax
import jax.numpy as jnp
from jax import lax
from jax.experimental import pallas as pl
from jax.experimental.pallas import tpu as pltpu
from jax.sharding import PartitionSpec as P

HEAD = 64
KV_HEADS = 4
BLOCK = 128
MESH = pl.DeviceIdType.MESH
CHUNKS = 2
F32, BF16 = jnp.float32, jnp.bfloat16


def kernel(
    chips,
    regions,
    queries,
    mold,
    q_weight,
    k_weight,
    v_weight,
    o_weight,
    lists,
    live,
    out,
    q_own,
    q_all,
    qw,
    kw,
    vw,
    wkv,
    ow,
    mold_own,
    mold_z,
    mold_c,
    kv_send,
    pool,
    kv_list,
    q_ext,
    scores,
    bias,
    attn,
    part,
    part_own,
    got,
    sem_local,
    mz_s,
    mz_r,
    mc_s,
    mc_r,
    kz_s,
    kz_r,
    kc_s,
    kc_r,
    ki_s,
    ki_r,
    kx_s,
    kx_r,
    qz_s,
    qz_r,
    qc_s,
    qc_r,
    ow_s,
    ow_r,
    ac_s,
    ac_r,
    oz_s,
    oz_r,
):
    region = lax.axis_index("region")
    shard = lax.axis_index("wshard")
    chip = shard // 2
    core = lax.rem(shard, 2)
    other = 1 - core
    odd = lax.rem(region, 2)
    qblocks, listed = lists.shape
    pool_blocks = pool.shape[0] // 3
    chip_blocks = pool_blocks // chips
    chip_rows = chip_blocks * BLOCK
    rows_j = chip_rows // CHUNKS
    half = rows_j // 2
    piece = half // BLOCK
    far = range(1, chips)
    near = range(chips)

    def ahead(d):
        return lax.rem(chip + d, chips)

    def behind(d):
        return lax.rem(chip + chips - d, chips)

    def z_peer(d):
        return (region, ahead(d) * 2 + core)

    core_peer = (region, chip * 2 + other)
    sibling = (region + 1 - 2 * odd, shard)
    x_to = (lax.rem(region + regions + 2 - 4 * odd, regions), shard)
    x_from = (lax.rem(region + regions - 2 + 4 * odd, regions), shard)

    def remote(src, dst, send, recv, peer):
        return pltpu.make_async_remote_copy(
            src_ref=src, dst_ref=dst, send_sem=send, recv_sem=recv, device_id=peer, device_id_type=MESH
        )

    local = [
        pltpu.make_async_copy(k_weight, kw, sem_local.at[0]),
        pltpu.make_async_copy(v_weight, vw, sem_local.at[1]),
        pltpu.make_async_copy(q_weight, qw, sem_local.at[2]),
        pltpu.make_async_copy(o_weight, ow.at[core], sem_local.at[3]),
        pltpu.make_async_copy(queries, q_own, sem_local.at[4]),
        pltpu.make_async_copy(
            mold.at[pl.ds(pl.multiple_of(chip * chip_rows, BLOCK), chip_rows)], mold_own, sem_local.at[5]
        ),
    ]
    for copy in (local[5], local[0], local[1], local[4], local[2], local[3]):
        copy.start()

    barrier = pltpu.get_barrier_semaphore()
    partners = [z_peer(d) for d in far] + [core_peer, sibling, x_to, x_from]
    for peer in partners:
        pl.semaphore_signal(barrier, inc=1, device_id=peer, device_id_type=MESH)
    pl.semaphore_wait(barrier, len(partners))

    def mold_z_copy(j, d):
        row = pl.multiple_of(ahead(d) * chip_rows + j * rows_j, BLOCK)
        return remote(
            mold.at[pl.ds(row, rows_j)], mold_z.at[j, d - 1], mz_s.at[j, d - 1], mz_r.at[j, d - 1], z_peer(d)
        )

    for j in range(CHUNKS):
        for d in far:
            mold_z_copy(j, d).start()

    def mold_src(j, d, side):
        rows = pl.ds(pl.multiple_of(side * half, BLOCK), half)
        if d == 0:
            return mold_own.at[pl.ds(pl.multiple_of(j * rows_j + side * half, BLOCK), half)]
        return mold_z.at[j, d - 1, rows]

    def mold_c_copy(j, d):
        return remote(mold_src(j, d, other), mold_c.at[j, d], mc_s.at[j, d], mc_r.at[j, d], core_peer)

    local[5].wait()
    for j in range(CHUNKS):
        mold_c_copy(j, 0).start()

    local[0].wait()
    local[1].wait()
    for h in range(KV_HEADS):
        cols = slice(h * HEAD, (h + 1) * HEAD)
        wkv[:, h * 2 * HEAD : (h + 1) * 2 * HEAD] = jnp.concatenate([kw[:, cols], vw[:, cols]], axis=1)

    def mark(i, _):
        for l in range(listed):
            repeat = jnp.int32(0)
            for e in range(l):
                repeat = jnp.where(lists[i, e] == lists[i, l], jnp.int32(1), repeat)
            bias[i, l] = jnp.where(repeat == 1, F32(-1e30), F32(0.0))
        return 0

    lax.fori_loop(0, qblocks, mark, 0)

    local[3].wait()
    ow_copy = remote(ow.at[core], ow.at[core], ow_s, ow_r, core_peer)
    ow_copy.start()

    def at_piece(slot, j, d, side):
        return pl.ds(slot * pool_blocks + behind(d) * chip_blocks + (j * 2 + side) * piece, piece)

    def kv_z_copy(j, d):
        spot = at_piece(0, j, 0, core)
        return remote(kv_send.at[j, ahead(d)], pool.at[spot], kz_s.at[j, d - 1], kz_r.at[j, d - 1], z_peer(d))

    def kv_z_got(j, d):
        spot = at_piece(0, j, d, core)
        return remote(kv_send.at[j, 0], pool.at[spot], kz_s.at[j, d - 1], kz_r.at[j, d - 1], z_peer(d))

    def kv_core(slot, j, d):
        spot = at_piece(slot, j, d, core)
        return remote(pool.at[spot], pool.at[spot], kc_s.at[slot, j, d], kc_r.at[slot, j, d], core_peer)

    def kv_core_got(slot, j, d):
        spot = at_piece(slot, j, d, other)
        return remote(pool.at[spot], pool.at[spot], kc_s.at[slot, j, d], kc_r.at[slot, j, d], core_peer)

    def kv_sib(j, d):
        return remote(
            pool.at[at_piece(0, j, d, core)],
            pool.at[at_piece(1, j, d, core)],
            ki_s.at[j, d],
            ki_r.at[j, d],
            sibling,
        )

    def kv_x(j, d):
        return remote(
            pool.at[at_piece(1, j, d, core)],
            pool.at[at_piece(2, j, d, core)],
            kx_s.at[j, d],
            kx_r.at[j, d],
            x_to,
        )

    def q_z_copy(d):
        return remote(queries, q_all.at[shard], qz_s.at[d - 1], qz_r.at[d - 1], z_peer(d))

    def q_z_got(d):
        return remote(queries, q_all.at[behind(d) * 2 + core], qz_s.at[d - 1], qz_r.at[d - 1], z_peer(d))

    def q_core(d):
        if d == 0:
            return remote(queries, q_all.at[shard], qc_s.at[0], qc_r.at[0], core_peer)
        slot = behind(d) * 2 + core
        return remote(q_all.at[slot], q_all.at[slot], qc_s.at[d], qc_r.at[d], core_peer)

    def q_core_got(d):
        slot = behind(d) * 2 + other
        return remote(queries, q_all.at[slot], qc_s.at[d], qc_r.at[d], core_peer)

    q_core(0).start()

    for j in range(CHUNKS):
        for d in far:
            mold_z_copy(j, d).wait_recv()
            mold_c_copy(j, d).start()
        total = jnp.zeros((half, wkv.shape[1]), F32)
        for d in near:
            depth = 2 * BLOCK
            base = pl.multiple_of(behind(d) * depth, depth)
            mine = wkv[pl.ds(pl.multiple_of(base + core * BLOCK, BLOCK), BLOCK), :]
            total += jnp.dot(mold_src(j, d, core)[...], mine, preferred_element_type=F32)
            mold_c_copy(j, d).wait_recv()
            theirs = wkv[pl.ds(pl.multiple_of(base + other * BLOCK, BLOCK), BLOCK), :]
            total += jnp.dot(mold_c[j, d], theirs, preferred_element_type=F32)
        pairs = total.astype(BF16)
        for h in range(KV_HEADS):
            kv_send[j, h] = pairs[:, h * BLOCK : (h + 1) * BLOCK].reshape(piece, BLOCK, BLOCK)
        pool[at_piece(0, j, 0, core)] = kv_send[j, chip]
        for d in far:
            kv_z_copy(j, d).start()
        kv_sib(j, 0).start()
        kv_core(0, j, 0).start()

    for d in far:
        q_z_copy(d).start()

    for j in range(CHUNKS):
        for d in far:
            kv_z_got(j, d).wait_recv()
            kv_sib(j, d).start()
            kv_core(0, j, d).start()
    for j in range(CHUNKS):
        for d in near:
            kv_sib(j, d).wait_recv()
            kv_x(j, d).start()
            kv_core(1, j, d).start()
    for d in far:
        q_z_got(d).wait_recv()
        q_core(d).start()
    for j in range(CHUNKS):
        for d in near:
            kv_x(j, d).wait_recv()
            kv_core(2, j, d).start()

    local[4].wait()
    local[2].wait()
    rows_q = q_own.shape[0]

    def weight_rows(s):
        return qw[pl.ds(pl.multiple_of(s * BLOCK, BLOCK), BLOCK), :]

    q_sum = jnp.dot(q_own[...], weight_rows(shard), preferred_element_type=F32)
    q_core_got(0).wait_recv()
    q_sum += jnp.dot(q_all[chip * 2 + other], weight_rows(chip * 2 + other), preferred_element_type=F32)
    for d in far:
        s = behind(d) * 2 + core
        q_sum += jnp.dot(q_all[s], weight_rows(s), preferred_element_type=F32)
        q_core_got(d).wait_recv()
        s = behind(d) * 2 + other
        q_sum += jnp.dot(q_all[s], weight_rows(s), preferred_element_type=F32)
    q_scaled = q_sum.astype(BF16).astype(F32) * HEAD**-0.5
    lane = lax.broadcasted_iota(jnp.int32, (rows_q, 2 * HEAD), 1)
    first = jnp.where(lane < HEAD, q_scaled, 0.0).astype(BF16)
    second = jnp.where(lane < HEAD, pltpu.roll(q_scaled, HEAD, 1), 0.0).astype(BF16)
    for i in range(qblocks):
        rows = slice(i * BLOCK, (i + 1) * BLOCK)
        q_ext[i, :BLOCK] = first[rows]
        q_ext[i, BLOCK:] = second[rows]

    for slot in range(3):
        for j in range(CHUNKS):
            for d in near:
                kv_core_got(slot, j, d).wait_recv()
    ow_copy.wait_recv()

    low = lax.broadcasted_iota(jnp.int32, (BLOCK, 2 * HEAD), 1) < HEAD
    wide = 2 * BLOCK

    def attn_copy(i):
        return remote(attn.at[core, i], attn.at[core, i], ac_s.at[i], ac_r.at[i], core_peer)

    def attn_got(i):
        return remote(attn.at[other, i], attn.at[other, i], ac_s.at[i], ac_r.at[i], core_peer)

    def part_copy(i, d):
        return remote(part.at[i, d - 1], got.at[i, d - 1], oz_s.at[i, d - 1], oz_r.at[i, d - 1], z_peer(d))

    def attend(i):
        for l in range(listed):
            block = lists[i, l]
            home = block // pool_blocks
            slot = jnp.where(home == region, 0, jnp.where(home == sibling[0], 1, 2))
            kv_list[l * BLOCK : (l + 1) * BLOCK] = pool[slot * pool_blocks + lax.rem(block, pool_blocks)]
        q = q_ext[i]
        top = jnp.full((wide, BLOCK), -jnp.inf, F32)
        for p in range(listed // 2):
            keys = kv_list[p * wide : (p + 1) * wide]
            s = lax.dot_general(q, keys, (((1,), (1,)), ((), ())), preferred_element_type=F32)
            for e in range(2):
                se = s[:, e * BLOCK : (e + 1) * BLOCK] + bias[i, 2 * p + e]
                scores[:, p * wide + e * BLOCK : p * wide + (e + 1) * BLOCK] = se
                top = jnp.maximum(top, se)
        top = jnp.max(top, axis=1, keepdims=True)
        total = jnp.zeros((wide, BLOCK), F32)
        mixed = jnp.zeros((wide, BLOCK), F32)
        for p in range(listed // 2):
            e = jnp.exp(scores[:, p * wide : (p + 1) * wide] - top)
            total += e[:, :BLOCK] + e[:, BLOCK:]
            mixed += jnp.dot(e.astype(BF16), kv_list[p * wide : (p + 1) * wide], preferred_element_type=F32)
        mixed = mixed / jnp.sum(total, axis=1, keepdims=True)
        both = jnp.where(low, pltpu.roll(mixed[:BLOCK], HEAD, 1), mixed[BLOCK:])
        attn[core, i] = jnp.where(i < live[0], both, 0.0).astype(BF16)
        attn_copy(i).start()

    def project(i):
        attn_got(i).wait_recv()
        for d in near:
            cols = pl.ds(pl.multiple_of((ahead(d) * 2 + core) * BLOCK, BLOCK), BLOCK)
            term = jnp.dot(attn[0, i], ow[0, :, cols], preferred_element_type=F32)
            term += jnp.dot(attn[1, i], ow[1, :, cols], preferred_element_type=F32)
            if d == 0:
                part_own[i] = term
            else:
                part[i, d - 1] = term.astype(BF16)
                part_copy(i, d).start()

    def step(i, _):
        attend(i)

        @pl.when(i > 0)
        def _():
            project(i - 1)

        return 0

    lax.fori_loop(0, qblocks, step, 0)
    project(qblocks - 1)

    def finish(i, _):
        term = part_own[i]
        for d in far:
            part_copy(i, d).wait_recv()
            term += got[i, d - 1].astype(F32)
        out[pl.ds(pl.multiple_of(i * BLOCK, BLOCK), BLOCK), :] = term.astype(BF16)
        return 0

    lax.fori_loop(0, qblocks, finish, 0)

    ow_copy.wait_send()
    for j in range(CHUNKS):
        for d in near:
            mold_c_copy(j, d).wait_send()
            kv_sib(j, d).wait_send()
            kv_x(j, d).wait_send()
            for slot in range(3):
                kv_core(slot, j, d).wait_send()
        for d in far:
            mold_z_copy(j, d).wait_send()
            kv_z_copy(j, d).wait_send()
    for d in far:
        q_z_copy(d).wait_send()
    for d in near:
        q_core(d).wait_send()
    for i in range(qblocks):
        attn_copy(i).wait_send()
        for d in far:
            part_copy(i, d).wait_send()


def solution(mesh):
    regions, shards = mesh.shape["region"], mesh.shape["wshard"]
    chips = shards // 2

    def step(queries, mold, q_weight, k_weight, v_weight, o_weight, lists, live):
        rows_q, feats = queries.shape
        rows_m = mold.shape[0]
        width, kv_cols = k_weight.shape
        qblocks, listed = lists.shape
        pool_blocks = rows_m // BLOCK
        rows_j = rows_m // chips // CHUNKS
        half = rows_j // 2
        piece = half // BLOCK
        far = chips - 1
        dma = pltpu.SemaphoreType.DMA
        any_space = pl.BlockSpec(memory_space=pl.ANY)
        smem = pl.BlockSpec(memory_space=pltpu.SMEM)
        scratch = [
            pltpu.VMEM((rows_q, feats), BF16),
            pltpu.VMEM((shards, rows_q, feats), BF16),
            pltpu.VMEM(q_weight.shape, BF16),
            pltpu.VMEM(k_weight.shape, BF16),
            pltpu.VMEM(v_weight.shape, BF16),
            pltpu.VMEM((width, 2 * kv_cols), BF16),
            pltpu.VMEM((2,) + o_weight.shape, BF16),
            pltpu.VMEM((rows_m // chips, feats), BF16),
            pltpu.VMEM((CHUNKS, far, rows_j, feats), BF16),
            pltpu.VMEM((CHUNKS, chips, half, feats), BF16),
            pltpu.VMEM((CHUNKS, KV_HEADS, piece, BLOCK, 2 * HEAD), BF16),
            pltpu.VMEM((3 * pool_blocks, BLOCK, 2 * HEAD), BF16),
            pltpu.VMEM((listed * BLOCK, 2 * HEAD), BF16),
            pltpu.VMEM((qblocks, 2 * BLOCK, 2 * HEAD), BF16),
            pltpu.VMEM((2 * BLOCK, listed * BLOCK), F32),
            pltpu.SMEM((qblocks, listed), F32),
            pltpu.VMEM((2, qblocks, BLOCK, 2 * HEAD), BF16),
            pltpu.VMEM((qblocks, far, BLOCK, feats), BF16),
            pltpu.VMEM((qblocks, BLOCK, feats), F32),
            pltpu.VMEM((qblocks, far, BLOCK, feats), BF16),
            dma((6,)),
        ]
        for shape in (
            (CHUNKS, far),
            (CHUNKS, chips),
            (CHUNKS, far),
            (3, CHUNKS, chips),
            (CHUNKS, chips),
            (CHUNKS, chips),
            (far,),
            (chips,),
            (),
            (qblocks,),
            (qblocks, far),
        ):
            scratch += [dma(shape), dma(shape)]
        return pl.pallas_call(
            functools.partial(kernel, chips, regions),
            out_shape=jax.ShapeDtypeStruct((rows_q, feats), BF16),
            in_specs=[any_space] * 6 + [smem] * 2,
            out_specs=pl.BlockSpec(memory_space=pltpu.VMEM),
            scratch_shapes=scratch,
            compiler_params=pltpu.CompilerParams(
                collective_id=0, has_side_effects=True, vmem_limit_bytes=40 << 20
            ),
        )(queries, mold, q_weight, k_weight, v_weight, o_weight, lists, live)

    return jax.shard_map(
        step,
        mesh=mesh,
        in_specs=(
            P("region", "wshard"),
            P("region", "wshard"),
            P(None, "wshard"),
            P(),
            P(),
            P("wshard", None),
            P("region", None),
            P("region"),
        ),
        out_specs=P("region", "wshard"),
        check_vma=False,
    )
```

```python
import functools

import jax
import jax.numpy as jnp
from jax import lax
from jax.experimental import pallas as pl
from jax.experimental.pallas import tpu as pltpu
from jax.sharding import PartitionSpec as P

HEAD = 64
KV_HEADS = 4
BLOCK = 128
MESH = pl.DeviceIdType.MESH
CHUNKS = 2
F32, BF16 = jnp.float32, jnp.bfloat16


def kernel(
    chips,
    regions,
    queries,
    mold,
    q_weight,
    k_weight,
    v_weight,
    o_weight,
    lists,
    live,
    out,
    q_feats,
    q_rows,
    q_send,
    qw,
    qwz,
    kw,
    vw,
    wkv,
    ow,
    mold_own,
    mold_z,
    mold_c,
    kv_send,
    pool,
    kv_list,
    q_ext,
    scores,
    bias,
    owz,
    attn,
    attn_got,
    part,
    part_got,
    out_send,
    sem_local,
    mz_s,
    mz_r,
    mc_s,
    mc_r,
    kz_s,
    kz_r,
    kc_s,
    kc_r,
    ki_s,
    ki_r,
    kx_s,
    kx_r,
    qz_s,
    qz_r,
    qc_s,
    qc_r,
    qh_s,
    qh_r,
    w1_s,
    w1_r,
    w2_s,
    w2_r,
    w3_s,
    w3_r,
    o1_s,
    o1_r,
    o2_s,
    o2_r,
    o3_s,
    o3_r,
    az_s,
    az_r,
    pc_s,
    pc_r,
    oz_s,
    oz_r,
):
    region = lax.axis_index("region")
    shard = lax.axis_index("wshard")
    chip = shard // 2
    core = lax.rem(shard, 2)
    other = 1 - core
    odd = lax.rem(region, 2)
    qblocks, listed = lists.shape
    pool_blocks = pool.shape[0] // 3
    chip_blocks = pool_blocks // chips
    chip_rows = chip_blocks * BLOCK
    rows_j = chip_rows // CHUNKS
    half = rows_j // 2
    piece = half // BLOCK
    far = range(1, chips)
    near = range(chips)

    def ahead(d):
        return lax.rem(chip + d, chips)

    def behind(d):
        return lax.rem(chip + chips - d, chips)

    def z_peer(d):
        return (region, ahead(d) * 2 + core)

    core_peer = (region, chip * 2 + other)
    sibling = (region + 1 - 2 * odd, shard)
    x_to = (lax.rem(region + regions + 2 - 4 * odd, regions), shard)
    x_from = (lax.rem(region + regions - 2 + 4 * odd, regions), shard)
    column = region // 2
    side_x = 4
    side_y = regions // 2 // side_x
    at_x = lax.rem(column, side_x)
    at_y = column // side_x
    share = qwz.shape[2]
    step_s = 1 + 2 * odd
    offsets = (0, step_s, chips - step_s, 2)

    def x_peer(e):
        return ((at_y * side_x + lax.rem(at_x + e, side_x)) * 2 + odd, shard)

    def y_peer(e):
        return ((lax.rem(at_y + e, side_y) * side_x + at_x) * 2 + odd, shard)

    def sib_peer(d):
        return (sibling[0], ahead(d) * 2 + core)

    def remote(src, dst, send, recv, peer):
        return pltpu.make_async_remote_copy(
            src_ref=src, dst_ref=dst, send_sem=send, recv_sem=recv, device_id=peer, device_id_type=MESH
        )

    local = [
        pltpu.make_async_copy(k_weight, kw, sem_local.at[0]),
        pltpu.make_async_copy(v_weight, vw, sem_local.at[1]),
        pltpu.make_async_copy(q_weight, qw, sem_local.at[2]),
        pltpu.make_async_copy(o_weight, ow, sem_local.at[3]),
        pltpu.make_async_copy(
            queries.at[pl.ds(pl.multiple_of(chip * BLOCK, BLOCK), BLOCK)], q_feats.at[shard], sem_local.at[4]
        ),
        pltpu.make_async_copy(
            mold.at[pl.ds(pl.multiple_of(chip * chip_rows, BLOCK), chip_rows)], mold_own, sem_local.at[5]
        ),
    ]
    for copy in (local[5], local[0], local[1], local[4], local[2], local[3]):
        copy.start()

    barrier = pltpu.get_barrier_semaphore()
    partners = [z_peer(d) for d in far] + [core_peer, sibling, x_to, x_from]
    partners += [sib_peer(chips - step_s), sib_peer(2)]
    partners += [x_peer(e) for e in range(1, side_x)] + [y_peer(e) for e in range(1, side_y)]
    for peer in partners:
        pl.semaphore_signal(barrier, inc=1, device_id=peer, device_id_type=MESH)
    pl.semaphore_wait(barrier, len(partners))

    def w1_copy(d):
        rows = pl.ds(pl.multiple_of(column * share, share), share)
        return remote(q_weight.at[rows], qwz.at[column, d - 1], w1_s.at[d - 1], w1_r.at[d - 1], z_peer(d))

    def w2_copy(e, sent):
        spot = column if sent else at_y * side_x + lax.rem(at_x + side_x - e, side_x)
        return remote(qwz.at[column], qwz.at[spot], w2_s.at[e - 1], w2_r.at[e - 1], x_peer(e))

    def w3_copy(e, sent):
        mine = pl.ds(at_y * side_x, side_x)
        spot = mine if sent else pl.ds(lax.rem(at_y + side_y - e, side_y) * side_x, side_x)
        return remote(qwz.at[mine], qwz.at[spot], w3_s.at[e - 1], w3_r.at[e - 1], y_peer(e))

    column_o = at_x * side_y + at_y

    def o1_copy(d):
        rows = pl.ds(pl.multiple_of(lax.rem(column_o, 2) * share, share), share)
        cols = pl.ds(pl.multiple_of(column_o // 2 * BLOCK, BLOCK), BLOCK)
        return remote(o_weight.at[rows, cols], owz.at[column_o, d - 1], o1_s.at[d - 1], o1_r.at[d - 1], z_peer(d))

    def o2_copy(e, sent):
        spot = column_o if sent else at_x * side_y + lax.rem(at_y + side_y - e, side_y)
        return remote(owz.at[column_o], owz.at[spot], o2_s.at[e - 1], o2_r.at[e - 1], y_peer(e))

    def o3_copy(e, sent):
        mine = pl.ds(at_x * side_y, side_y)
        spot = mine if sent else pl.ds(lax.rem(at_x + side_x - e, side_x) * side_y, side_y)
        return remote(owz.at[mine], owz.at[spot], o3_s.at[e - 1], o3_r.at[e - 1], x_peer(e))

    for d in far:
        w1_copy(d).start()
    for d in far:
        o1_copy(d).start()

    def mold_z_copy(j, d):
        row = pl.multiple_of(ahead(d) * chip_rows + j * rows_j, BLOCK)
        return remote(
            mold.at[pl.ds(row, rows_j)], mold_z.at[j, d - 1], mz_s.at[j, d - 1], mz_r.at[j, d - 1], z_peer(d)
        )

    for j in range(CHUNKS):
        for d in far:
            mold_z_copy(j, d).start()

    def mold_src(j, d, side):
        rows = pl.ds(pl.multiple_of(side * half, BLOCK), half)
        if d == 0:
            return mold_own.at[pl.ds(pl.multiple_of(j * rows_j + side * half, BLOCK), half)]
        return mold_z.at[j, d - 1, rows]

    def mold_c_copy(j, d):
        return remote(mold_src(j, d, other), mold_c.at[j, d], mc_s.at[j, d], mc_r.at[j, d], core_peer)

    local[5].wait()
    for j in range(CHUNKS):
        mold_c_copy(j, 0).start()

    local[0].wait()
    local[1].wait()
    for h in range(KV_HEADS):
        cols = slice(h * HEAD, (h + 1) * HEAD)
        wkv[:, h * 2 * HEAD : (h + 1) * 2 * HEAD] = jnp.concatenate([kw[:, cols], vw[:, cols]], axis=1)

    def mark(i, _):
        for l in range(listed):
            repeat = jnp.int32(0)
            for e in range(l):
                repeat = jnp.where(lists[i, e] == lists[i, l], jnp.int32(1), repeat)
            bias[i, l] = jnp.where(repeat == 1, F32(-1e30), F32(0.0))
        return 0

    lax.fori_loop(0, qblocks, mark, 0)

    def at_piece(slot, j, off, side):
        return pl.ds(slot * pool_blocks + behind(off) * chip_blocks + (j * 2 + side) * piece, piece)

    z_routes = ((step_s, 0), (chips - step_s, 1), (2, 1))
    z_arrivals = ((0, 1), (1, 1), (1, 3))

    def kv_z_copy(j, t):
        d, slot = z_routes[t]
        peer = sib_peer(d) if slot else z_peer(d)
        spot = at_piece(slot, j, 0, core)
        return remote(kv_send.at[j, ahead(d)], pool.at[spot], kz_s.at[j, t], kz_r.at[j, t], peer)

    def kv_z_got(j, t):
        slot, at = z_arrivals[t]
        spot = at_piece(slot, j, offsets[at], core)
        return remote(kv_send.at[j, 0], pool.at[spot], kz_s.at[j, t], kz_r.at[j, t], sibling)

    def kv_core(slot, j, t):
        spot = at_piece(slot, j, offsets[t], core)
        return remote(pool.at[spot], pool.at[spot], kc_s.at[slot, j, t], kc_r.at[slot, j, t], core_peer)

    def kv_core_got(slot, j, t):
        spot = at_piece(slot, j, offsets[t], other)
        return remote(pool.at[spot], pool.at[spot], kc_s.at[slot, j, t], kc_r.at[slot, j, t], core_peer)

    sib_sent = ((0, 0), (0, 1), (1, 1), (1, 3))
    sib_arrivals = ((1, 0), (1, 2), (0, 2), (0, 3))

    def kv_sib(j, t):
        slot, at = sib_sent[t]
        src = at_piece(slot, j, offsets[at], core)
        dst = at_piece(1 - slot, j, offsets[at], core)
        return remote(pool.at[src], pool.at[dst], ki_s.at[j, t], ki_r.at[j, t], sibling)

    def kv_sib_got(j, t):
        slot, at = sib_arrivals[t]
        spot = at_piece(slot, j, offsets[at], core)
        return remote(pool.at[spot], pool.at[spot], ki_s.at[j, t], ki_r.at[j, t], sibling)

    def kv_x(j, t):
        return remote(
            pool.at[at_piece(1, j, offsets[t], core)],
            pool.at[at_piece(2, j, offsets[t], core)],
            kx_s.at[j, t],
            kx_r.at[j, t],
            x_to,
        )

    def q_z_copy(d):
        rows = pl.ds(pl.multiple_of(ahead(d) * BLOCK, BLOCK), BLOCK)
        return remote(queries.at[rows], q_feats.at[shard], qz_s.at[d - 1], qz_r.at[d - 1], z_peer(d))

    def q_z_got(d):
        return remote(q_send.at[0], q_feats.at[behind(d) * 2 + core], qz_s.at[d - 1], qz_r.at[d - 1], z_peer(d))

    def q_core(d):
        spot = q_feats.at[behind(d) * 2 + core]
        return remote(spot, spot, qc_s.at[d], qc_r.at[d], core_peer)

    def q_core_got(d):
        spot = q_feats.at[behind(d) * 2 + other]
        return remote(spot, spot, qc_s.at[d], qc_r.at[d], core_peer)

    def q_heads(d):
        return remote(q_send.at[d - 1], q_rows.at[chip], qh_s.at[d - 1], qh_r.at[d - 1], z_peer(d))

    def q_heads_got(d):
        return remote(q_send.at[d - 1], q_rows.at[behind(d)], qh_s.at[d - 1], qh_r.at[d - 1], z_peer(d))

    local[4].wait()
    q_core(0).start()
    for d in far:
        w1_copy(d).wait_recv()
    for e in range(1, side_x):
        w2_copy(e, True).start()
    for d in far:
        o1_copy(d).wait_recv()
    for e in range(1, side_y):
        o2_copy(e, True).start()
    for e in range(1, side_x):
        w2_copy(e, False).wait_recv()
    for e in range(1, side_y):
        w3_copy(e, True).start()
    for e in range(1, side_y):
        o2_copy(e, False).wait_recv()
    for e in range(1, side_x):
        o3_copy(e, True).start()

    for j in range(CHUNKS):
        for d in far:
            mold_z_copy(j, d).wait_recv()
            mold_c_copy(j, d).start()
        total = jnp.zeros((half, wkv.shape[1]), F32)
        for d in near:
            depth = 2 * BLOCK
            base = pl.multiple_of(behind(d) * depth, depth)
            mine = wkv[pl.ds(pl.multiple_of(base + core * BLOCK, BLOCK), BLOCK), :]
            total += jnp.dot(mold_src(j, d, core)[...], mine, preferred_element_type=F32)
            mold_c_copy(j, d).wait_recv()
            theirs = wkv[pl.ds(pl.multiple_of(base + other * BLOCK, BLOCK), BLOCK), :]
            total += jnp.dot(mold_c[j, d], theirs, preferred_element_type=F32)
        pairs = total.astype(BF16)
        for h in range(KV_HEADS):
            kv_send[j, h] = pairs[:, h * BLOCK : (h + 1) * BLOCK].reshape(piece, BLOCK, BLOCK)
        pool[at_piece(0, j, 0, core)] = kv_send[j, chip]
        for t in range(3):
            kv_z_copy(j, t).start()
        kv_sib(j, 0).start()
        kv_core(0, j, 0).start()
        if j == 0:
            for d in far:
                q_z_copy(d).start()

    def forward(j):
        for t in range(3):
            kv_z_got(j, t).wait_recv()
            slot, at = z_arrivals[t]
            kv_sib(j, t + 1).start()
            if slot == 1:
                kv_x(j, at).start()
            kv_core(slot, j, at).start()

    forward(0)

    local[2].wait()
    for d in far:
        q_z_got(d).wait_recv()
        q_core(d).start()
    for e in range(1, side_y):
        w3_copy(e, False).wait_recv()
    for d in near:
        q_core_got(d).wait_recv()
    feats = jnp.concatenate([q_feats[f] for f in range(q_feats.shape[0])], axis=1)

    def project_q(weight):
        value = jnp.dot(feats, weight, preferred_element_type=F32).astype(BF16)
        return (value.astype(F32) * HEAD**-0.5).astype(BF16)

    for d in far:
        q_send[d - 1] = project_q(qwz[:, chips - d - 1].reshape(qw.shape))
        q_heads(d).start()
    q_rows[chip] = project_q(qw[...])

    for j in range(1, CHUNKS):
        forward(j)
    for j in range(CHUNKS):
        for t in range(4):
            kv_sib_got(j, t).wait_recv()
            slot, at = sib_arrivals[t]
            if slot == 1:
                kv_x(j, at).start()
            kv_core(slot, j, at).start()

    lane = lax.broadcasted_iota(jnp.int32, (BLOCK, 2 * HEAD), 1)
    for d in far:
        q_heads_got(d).wait_recv()
    for i in range(qblocks):
        value = q_rows[i].astype(F32)
        q_ext[i, :BLOCK] = jnp.where(lane < HEAD, value, 0.0).astype(BF16)
        q_ext[i, BLOCK:] = jnp.where(lane < HEAD, pltpu.roll(value, HEAD, 1), 0.0).astype(BF16)

    for j in range(CHUNKS):
        for t in (1, 3, 0, 2):
            kv_x(j, t).wait_recv()
            kv_core(2, j, t).start()

    for slot in range(3):
        for j in range(CHUNKS):
            for d in near:
                kv_core_got(slot, j, d).wait_recv()
    for e in range(1, side_x):
        o3_copy(e, False).wait_recv()
    local[3].wait()

    low = lax.broadcasted_iota(jnp.int32, (BLOCK, 2 * HEAD), 1) < HEAD
    wide = 2 * BLOCK

    def attn_copy(t):
        return remote(attn.at[t], attn_got.at[t - 1], az_s.at[t - 1], az_r.at[t - 1], z_peer(t))

    part_copy = remote(part, part_got, pc_s, pc_r, core_peer)

    def out_copy(d):
        rows = pl.ds(pl.multiple_of(chip * BLOCK, BLOCK), BLOCK)
        return remote(out_send.at[d - 1], out.at[rows], oz_s.at[d - 1], oz_r.at[d - 1], z_peer(d))

    def out_got(d):
        rows = pl.ds(pl.multiple_of(behind(d) * BLOCK, BLOCK), BLOCK)
        return remote(out_send.at[d - 1], out.at[rows], oz_s.at[d - 1], oz_r.at[d - 1], z_peer(d))

    def attend(t):
        i = ahead(t)
        for l in range(listed):
            block = lists[i, l]
            home = block // pool_blocks
            slot = jnp.where(home == region, 0, jnp.where(home == sibling[0], 1, 2))
            kv_list[l * BLOCK : (l + 1) * BLOCK] = pool[slot * pool_blocks + lax.rem(block, pool_blocks)]
        q = q_ext[i]
        top = jnp.full((wide, BLOCK), -jnp.inf, F32)
        for p in range(listed // 2):
            keys = kv_list[p * wide : (p + 1) * wide]
            s = lax.dot_general(q, keys, (((1,), (1,)), ((), ())), preferred_element_type=F32)
            for e in range(2):
                se = s[:, e * BLOCK : (e + 1) * BLOCK] + bias[i, 2 * p + e]
                scores[:, p * wide + e * BLOCK : p * wide + (e + 1) * BLOCK] = se
                top = jnp.maximum(top, se)
        top = jnp.max(top, axis=1, keepdims=True)
        total = jnp.zeros((wide, BLOCK), F32)
        mixed = jnp.zeros((wide, BLOCK), F32)
        for p in range(listed // 2):
            e = jnp.exp(scores[:, p * wide : (p + 1) * wide] - top)
            total += e[:, :BLOCK] + e[:, BLOCK:]
            mixed += jnp.dot(e.astype(BF16), kv_list[p * wide : (p + 1) * wide], preferred_element_type=F32)
        mixed = mixed / jnp.sum(total, axis=1, keepdims=True)
        both = jnp.where(low, pltpu.roll(mixed[:BLOCK], HEAD, 1), mixed[BLOCK:])
        attn[t] = jnp.where(i < live[0], both, 0.0).astype(BF16)

    def step(u, _):
        t = lax.rem(u + 1, chips)
        attend(t)

        @pl.when(u < chips - 1)
        def _():
            attn_copy(t).start()

        return 0

    lax.fori_loop(0, qblocks, step, 0)

    for d in far:
        attn_copy(d).wait_recv()
    heads = jnp.concatenate([attn[0]] + [attn_got[d - 1] for d in far], axis=1)

    def project(block):
        cols = pl.ds(pl.multiple_of(block * BLOCK, BLOCK), BLOCK)
        weight = jnp.concatenate(
            [ow[:, cols]] + [owz[pl.ds(block * 2, 2), d - 1].reshape(BLOCK, BLOCK) for d in far], axis=0
        )
        return jnp.dot(heads, weight, preferred_element_type=F32)

    for d in near:
        part[d] = project(ahead(d) * 2 + other).astype(BF16)
    part_copy.start()
    terms = [project(ahead(d) * 2 + core) for d in near]
    part_copy.wait_recv()
    for d in far:
        out_send[d - 1] = (terms[d] + part_got[d].astype(F32)).astype(BF16)
        out_copy(d).start()
    rows = pl.ds(pl.multiple_of(chip * BLOCK, BLOCK), BLOCK)
    out[rows, :] = (terms[0] + part_got[0].astype(F32)).astype(BF16)
    for d in far:
        out_got(d).wait_recv()

    part_copy.wait_send()
    for d in far:
        attn_copy(d).wait_send()
        out_copy(d).wait_send()
        o1_copy(d).wait_send()
    for e in range(1, side_y):
        o2_copy(e, True).wait_send()
    for e in range(1, side_x):
        o3_copy(e, True).wait_send()
    for j in range(CHUNKS):
        for d in near:
            mold_c_copy(j, d).wait_send()
            kv_sib(j, d).wait_send()
            kv_x(j, d).wait_send()
            for slot in range(3):
                kv_core(slot, j, d).wait_send()
        for d in far:
            mold_z_copy(j, d).wait_send()
        for t in range(3):
            kv_z_copy(j, t).wait_send()
    for d in far:
        w1_copy(d).wait_send()
        q_z_copy(d).wait_send()
        q_heads(d).wait_send()
    for e in range(1, side_x):
        w2_copy(e, True).wait_send()
    for e in range(1, side_y):
        w3_copy(e, True).wait_send()
    for d in near:
        q_core(d).wait_send()


def solution(mesh):
    regions, shards = mesh.shape["region"], mesh.shape["wshard"]
    chips = shards // 2

    def step(queries, mold, q_weight, k_weight, v_weight, o_weight, lists, live):
        rows_q, feats = queries.shape
        rows_m = mold.shape[0]
        width, kv_cols = k_weight.shape
        qblocks, listed = lists.shape
        pool_blocks = rows_m // BLOCK
        rows_j = rows_m // chips // CHUNKS
        half = rows_j // 2
        piece = half // BLOCK
        far = chips - 1
        columns = regions // 2
        dma = pltpu.SemaphoreType.DMA
        any_space = pl.BlockSpec(memory_space=pl.ANY)
        smem = pl.BlockSpec(memory_space=pltpu.SMEM)
        scratch = [
            pltpu.VMEM((shards, BLOCK, feats), BF16),
            pltpu.VMEM((chips, BLOCK, feats), BF16),
            pltpu.VMEM((far, BLOCK, feats), BF16),
            pltpu.VMEM(q_weight.shape, BF16),
            pltpu.VMEM((columns, far, width // columns, feats), BF16),
            pltpu.VMEM(k_weight.shape, BF16),
            pltpu.VMEM(v_weight.shape, BF16),
            pltpu.VMEM((width, 2 * kv_cols), BF16),
            pltpu.VMEM(o_weight.shape, BF16),
            pltpu.VMEM((rows_m // chips, feats), BF16),
            pltpu.VMEM((CHUNKS, far, rows_j, feats), BF16),
            pltpu.VMEM((CHUNKS, chips, half, feats), BF16),
            pltpu.VMEM((CHUNKS, KV_HEADS, piece, BLOCK, 2 * HEAD), BF16),
            pltpu.VMEM((3 * pool_blocks, BLOCK, 2 * HEAD), BF16),
            pltpu.VMEM((listed * BLOCK, 2 * HEAD), BF16),
            pltpu.VMEM((qblocks, 2 * BLOCK, 2 * HEAD), BF16),
            pltpu.VMEM((2 * BLOCK, listed * BLOCK), F32),
            pltpu.SMEM((qblocks, listed), F32),
            pltpu.VMEM((columns, far, width // columns, feats), BF16),
            pltpu.VMEM((chips, BLOCK, 2 * HEAD), BF16),
            pltpu.VMEM((far, BLOCK, 2 * HEAD), BF16),
            pltpu.VMEM((chips, BLOCK, feats), BF16),
            pltpu.VMEM((chips, BLOCK, feats), BF16),
            pltpu.VMEM((far, BLOCK, feats), BF16),
            dma((6,)),
        ]
        for shape in (
            (CHUNKS, far),
            (CHUNKS, chips),
            (CHUNKS, 3),
            (3, CHUNKS, chips),
            (CHUNKS, chips),
            (CHUNKS, chips),
            (far,),
            (chips,),
            (far,),
            (far,),
            (3,),
            (regions // 8 - 1,),
            (far,),
            (regions // 8 - 1,),
            (3,),
            (far,),
            (),
            (far,),
        ):
            scratch += [dma(shape), dma(shape)]
        return pl.pallas_call(
            functools.partial(kernel, chips, regions),
            out_shape=jax.ShapeDtypeStruct((rows_q, feats), BF16),
            in_specs=[any_space] * 6 + [smem] * 2,
            out_specs=pl.BlockSpec(memory_space=pltpu.VMEM),
            scratch_shapes=scratch,
            compiler_params=pltpu.CompilerParams(
                collective_id=0, has_side_effects=True, vmem_limit_bytes=60 << 20
            ),
        )(queries, mold, q_weight, k_weight, v_weight, o_weight, lists, live)

    return jax.shard_map(
        step,
        mesh=mesh,
        in_specs=(
            P("region", "wshard"),
            P("region", "wshard"),
            P(None, "wshard"),
            P(),
            P(),
            P("wshard", None),
            P("region", None),
            P("region"),
        ),
        out_specs=P("region", "wshard"),
        check_vma=False,
    )
```

```python
import functools

import jax
import jax.numpy as jnp
from jax import lax
from jax.experimental import pallas as pl
from jax.experimental.pallas import tpu as pltpu
from jax.sharding import PartitionSpec as P

HEAD = 64
KV_HEADS = 4
BLOCK = 128
MESH = pl.DeviceIdType.MESH
CHUNKS = 2
F32, BF16 = jnp.float32, jnp.bfloat16


def kernel(
    chips,
    regions,
    queries,
    mold,
    q_weight,
    k_weight,
    v_weight,
    o_weight,
    lists,
    live,
    out,
    q_own,
    q_feats,
    q_rows,
    q_send,
    qw,
    qwz,
    kw,
    vw,
    wkv,
    ow,
    mold_own,
    mold_z,
    mold_c,
    kv_send,
    pool,
    kv_list,
    q_ext,
    scores,
    keep,
    owz,
    attn,
    attn_got,
    part,
    part_got,
    out_send,
    sem_local,
    mz_s,
    mz_r,
    mc_s,
    mc_r,
    kz_s,
    kz_r,
    kc_s,
    kc_r,
    ki_s,
    ki_r,
    kx_s,
    kx_r,
    qz_s,
    qz_r,
    qc_s,
    qc_r,
    qh_s,
    qh_r,
    w1_s,
    w1_r,
    w2_s,
    w2_r,
    w3_s,
    w3_r,
    o1_s,
    o1_r,
    o2_s,
    o2_r,
    o3_s,
    o3_r,
    az_s,
    az_r,
    pc_s,
    pc_r,
    oz_s,
    oz_r,
):
    region = lax.axis_index("region")
    shard = lax.axis_index("wshard")
    chip = shard // 2
    core = lax.rem(shard, 2)
    other = 1 - core
    odd = lax.rem(region, 2)
    qblocks, listed = lists.shape
    pool_blocks = pool.shape[0] // 3
    chip_blocks = pool_blocks // chips
    chip_rows = chip_blocks * BLOCK
    rows_j = chip_rows // CHUNKS
    half = rows_j // 2
    piece = half // BLOCK
    far = range(1, chips)
    near = range(chips)

    def ahead(d):
        return lax.rem(chip + d, chips)

    def behind(d):
        return lax.rem(chip + chips - d, chips)

    def z_peer(d):
        return (region, ahead(d) * 2 + core)

    core_peer = (region, chip * 2 + other)
    sibling = (region + 1 - 2 * odd, shard)
    x_to = (lax.rem(region + regions + 2 - 4 * odd, regions), shard)
    x_from = (lax.rem(region + regions - 2 + 4 * odd, regions), shard)
    column = region // 2
    side_x = 4
    side_y = regions // 2 // side_x
    at_x = lax.rem(column, side_x)
    at_y = column // side_x
    share = qwz.shape[2]
    step_s = 1 + 2 * odd
    offsets = (0, step_s, chips - step_s, 2)

    def x_peer(e):
        return ((at_y * side_x + lax.rem(at_x + e, side_x)) * 2 + odd, shard)

    def y_peer(e):
        return ((lax.rem(at_y + e, side_y) * side_x + at_x) * 2 + odd, shard)

    def sib_peer(d):
        return (sibling[0], ahead(d) * 2 + core)

    def remote(src, dst, send, recv, peer):
        return pltpu.make_async_remote_copy(
            src_ref=src, dst_ref=dst, send_sem=send, recv_sem=recv, device_id=peer, device_id_type=MESH
        )

    local = [
        pltpu.make_async_copy(k_weight, kw, sem_local.at[0]),
        pltpu.make_async_copy(v_weight, vw, sem_local.at[1]),
        pltpu.make_async_copy(q_weight, qw, sem_local.at[2]),
        pltpu.make_async_copy(o_weight, ow, sem_local.at[3]),
        pltpu.make_async_copy(queries, q_own, sem_local.at[4]),
        pltpu.make_async_copy(mold, mold_own, sem_local.at[5]),
    ]
    for copy in (local[5], local[2], local[3], local[0], local[1], local[4]):
        copy.start()

    barrier = pltpu.get_barrier_semaphore()
    partners = [z_peer(d) for d in far] + [core_peer, sibling, x_to, x_from]
    partners += [sib_peer(chips - step_s), sib_peer(2)]
    partners += [x_peer(e) for e in range(1, side_x)] + [y_peer(e) for e in range(1, side_y)]
    for peer in partners:
        pl.semaphore_signal(barrier, inc=1, device_id=peer, device_id_type=MESH)
    for copy in local:
        copy.wait()
    q_feats[shard] = q_own[pl.ds(pl.multiple_of(chip * BLOCK, BLOCK), BLOCK), :]
    for h in range(KV_HEADS):
        cols = slice(h * HEAD, (h + 1) * HEAD)
        wkv[:, h * 2 * HEAD : (h + 1) * 2 * HEAD] = jnp.concatenate([kw[:, cols], vw[:, cols]], axis=1)

    def mark(i, _):
        for l in range(listed):
            repeat = jnp.int32(0)
            for e in range(l):
                repeat = jnp.where(lists[i, e] == lists[i, l], jnp.int32(1), repeat)
            keep[i, l] = jnp.where(repeat == 1, F32(0.0), F32(1.0))
        return 0

    lax.fori_loop(0, qblocks, mark, 0)

    pl.semaphore_wait(barrier, len(partners))

    def w1_copy(d):
        rows = pl.ds(pl.multiple_of(column * share, share), share)
        return remote(qw.at[rows], qwz.at[column, d - 1], w1_s.at[d - 1], w1_r.at[d - 1], z_peer(d))

    def w2_copy(e, sent):
        spot = column if sent else at_y * side_x + lax.rem(at_x + side_x - e, side_x)
        return remote(qwz.at[column], qwz.at[spot], w2_s.at[e - 1], w2_r.at[e - 1], x_peer(e))

    def w3_copy(e, sent):
        mine = pl.ds(at_y * side_x, side_x)
        spot = mine if sent else pl.ds(lax.rem(at_y + side_y - e, side_y) * side_x, side_x)
        return remote(qwz.at[mine], qwz.at[spot], w3_s.at[e - 1], w3_r.at[e - 1], y_peer(e))

    column_o = at_x * side_y + at_y

    def o1_copy(d):
        rows = pl.ds(pl.multiple_of(lax.rem(column_o, 2) * share, share), share)
        cols = pl.ds(pl.multiple_of(column_o // 2 * BLOCK, BLOCK), BLOCK)
        return remote(ow.at[rows, cols], owz.at[column_o, d - 1], o1_s.at[d - 1], o1_r.at[d - 1], z_peer(d))

    def o2_copy(e, sent):
        spot = column_o if sent else at_x * side_y + lax.rem(at_y + side_y - e, side_y)
        return remote(owz.at[column_o], owz.at[spot], o2_s.at[e - 1], o2_r.at[e - 1], y_peer(e))

    def o3_copy(e, sent):
        mine = pl.ds(at_x * side_y, side_y)
        spot = mine if sent else pl.ds(lax.rem(at_x + side_x - e, side_x) * side_y, side_y)
        return remote(owz.at[mine], owz.at[spot], o3_s.at[e - 1], o3_r.at[e - 1], x_peer(e))

    for d in far:
        w1_copy(d).start()
    for d in far:
        o1_copy(d).start()

    def mold_z_copy(j, d):
        row = pl.multiple_of(ahead(d) * chip_rows + j * rows_j, BLOCK)
        return remote(
            mold_own.at[pl.ds(row, rows_j)], mold_z.at[j, d - 1], mz_s.at[j, d - 1], mz_r.at[j, d - 1], z_peer(d)
        )

    for j in range(CHUNKS):
        for d in far:
            mold_z_copy(j, d).start()

    def mold_src(j, d, side):
        rows = pl.ds(pl.multiple_of(side * half, BLOCK), half)
        if d == 0:
            return mold_own.at[pl.ds(pl.multiple_of(chip * chip_rows + j * rows_j + side * half, BLOCK), half)]
        return mold_z.at[j, d - 1, rows]

    def mold_c_copy(j, d):
        return remote(mold_src(j, d, other), mold_c.at[j, d], mc_s.at[j, d], mc_r.at[j, d], core_peer)

    for j in range(CHUNKS):
        mold_c_copy(j, 0).start()

    def at_piece(slot, j, off, side):
        return pl.ds(slot * pool_blocks + behind(off) * chip_blocks + (j * 2 + side) * piece, piece)

    z_routes = ((step_s, 0), (chips - step_s, 1), (2, 1))
    z_arrivals = ((0, 1), (1, 1), (1, 3))

    def kv_z_copy(j, t):
        d, slot = z_routes[t]
        peer = sib_peer(d) if slot else z_peer(d)
        spot = at_piece(slot, j, 0, core)
        return remote(kv_send.at[j, ahead(d)], pool.at[spot], kz_s.at[j, t], kz_r.at[j, t], peer)

    def kv_z_got(j, t):
        slot, at = z_arrivals[t]
        spot = at_piece(slot, j, offsets[at], core)
        return remote(kv_send.at[j, 0], pool.at[spot], kz_s.at[j, t], kz_r.at[j, t], sibling)

    def kv_core(slot, j, t):
        spot = at_piece(slot, j, offsets[t], core)
        return remote(pool.at[spot], pool.at[spot], kc_s.at[slot, j, t], kc_r.at[slot, j, t], core_peer)

    def kv_core_got(slot, j, t):
        spot = at_piece(slot, j, offsets[t], other)
        return remote(pool.at[spot], pool.at[spot], kc_s.at[slot, j, t], kc_r.at[slot, j, t], core_peer)

    sib_sent = ((0, 0), (0, 1), (1, 1), (1, 3))
    sib_arrivals = ((1, 0), (1, 2), (0, 2), (0, 3))

    def kv_sib(j, t):
        slot, at = sib_sent[t]
        src = at_piece(slot, j, offsets[at], core)
        dst = at_piece(1 - slot, j, offsets[at], core)
        return remote(pool.at[src], pool.at[dst], ki_s.at[j, t], ki_r.at[j, t], sibling)

    def kv_sib_got(j, t):
        slot, at = sib_arrivals[t]
        spot = at_piece(slot, j, offsets[at], core)
        return remote(pool.at[spot], pool.at[spot], ki_s.at[j, t], ki_r.at[j, t], sibling)

    def kv_x(j, t):
        return remote(
            pool.at[at_piece(1, j, offsets[t], core)],
            pool.at[at_piece(2, j, offsets[t], core)],
            kx_s.at[j, t],
            kx_r.at[j, t],
            x_to,
        )

    def q_z_copy(d):
        rows = pl.ds(pl.multiple_of(ahead(d) * BLOCK, BLOCK), BLOCK)
        return remote(q_own.at[rows], q_feats.at[shard], qz_s.at[d - 1], qz_r.at[d - 1], z_peer(d))

    def q_z_got(d):
        return remote(q_send.at[0], q_feats.at[behind(d) * 2 + core], qz_s.at[d - 1], qz_r.at[d - 1], z_peer(d))

    def q_core(d):
        spot = q_feats.at[behind(d) * 2 + core]
        return remote(spot, spot, qc_s.at[d], qc_r.at[d], core_peer)

    def q_core_got(d):
        spot = q_feats.at[behind(d) * 2 + other]
        return remote(spot, spot, qc_s.at[d], qc_r.at[d], core_peer)

    def q_heads(d):
        return remote(q_send.at[d - 1], q_rows.at[chip], qh_s.at[d - 1], qh_r.at[d - 1], z_peer(d))

    def q_heads_got(d):
        return remote(q_send.at[d - 1], q_rows.at[behind(d)], qh_s.at[d - 1], qh_r.at[d - 1], z_peer(d))

    q_core(0).start()
    for d in far:
        w1_copy(d).wait_recv()
    for e in range(1, side_x):
        w2_copy(e, True).start()
    for d in far:
        o1_copy(d).wait_recv()
    for e in range(1, side_y):
        o2_copy(e, True).start()
    for e in range(1, side_x):
        w2_copy(e, False).wait_recv()
    for e in range(1, side_y):
        w3_copy(e, True).start()
    for e in range(1, side_y):
        o2_copy(e, False).wait_recv()
    for e in range(1, side_x):
        o3_copy(e, True).start()

    for j in range(CHUNKS):
        for d in far:
            mold_z_copy(j, d).wait_recv()
            mold_c_copy(j, d).start()
        total = jnp.zeros((half, wkv.shape[1]), F32)
        for d in near:
            depth = 2 * BLOCK
            base = pl.multiple_of(behind(d) * depth, depth)
            mine = wkv[pl.ds(pl.multiple_of(base + core * BLOCK, BLOCK), BLOCK), :]
            total += jnp.dot(mold_src(j, d, core)[...], mine, preferred_element_type=F32)
            mold_c_copy(j, d).wait_recv()
            theirs = wkv[pl.ds(pl.multiple_of(base + other * BLOCK, BLOCK), BLOCK), :]
            total += jnp.dot(mold_c[j, d], theirs, preferred_element_type=F32)
        pairs = total.astype(BF16)
        for h in range(KV_HEADS):
            kv_send[j, h] = pairs[:, h * BLOCK : (h + 1) * BLOCK].reshape(piece, BLOCK, BLOCK)
        pool[at_piece(0, j, 0, core)] = kv_send[j, chip]
        for t in range(3):
            kv_z_copy(j, t).start()
        kv_sib(j, 0).start()
        kv_core(0, j, 0).start()
        if j == 0:
            for d in far:
                q_z_copy(d).start()

    def forward(j):
        for t in range(3):
            kv_z_got(j, t).wait_recv()
            slot, at = z_arrivals[t]
            kv_sib(j, t + 1).start()
            if slot == 1:
                kv_x(j, at).start()
            kv_core(slot, j, at).start()

    forward(0)

    for d in far:
        q_z_got(d).wait_recv()
        q_core(d).start()
    for e in range(1, side_y):
        w3_copy(e, False).wait_recv()
    for d in near:
        q_core_got(d).wait_recv()
    feats = jnp.concatenate([q_feats[f] for f in range(q_feats.shape[0])], axis=1)

    def project_q(weight):
        value = jnp.dot(feats, weight, preferred_element_type=F32).astype(BF16)
        return (value.astype(F32) * HEAD**-0.5).astype(BF16)

    for d in far:
        q_send[d - 1] = project_q(qwz[:, chips - d - 1].reshape(qw.shape))
        q_heads(d).start()
    q_rows[chip] = project_q(qw[...])

    for j in range(1, CHUNKS):
        forward(j)
    for j in range(CHUNKS):
        for t in range(4):
            kv_sib_got(j, t).wait_recv()
            slot, at = sib_arrivals[t]
            if slot == 1:
                kv_x(j, at).start()
            kv_core(slot, j, at).start()

    lane = lax.broadcasted_iota(jnp.int32, (BLOCK, 2 * HEAD), 1)
    for d in far:
        q_heads_got(d).wait_recv()
    for i in range(qblocks):
        value = q_rows[i].astype(F32)
        q_ext[i, :BLOCK] = jnp.where(lane < HEAD, value, 0.0).astype(BF16)
        q_ext[i, BLOCK:] = jnp.where(lane < HEAD, pltpu.roll(value, HEAD, 1), 0.0).astype(BF16)

    for j in range(CHUNKS):
        for t in (1, 3, 0, 2):
            kv_x(j, t).wait_recv()
            kv_core(2, j, t).start()

    for slot in range(3):
        for j in range(CHUNKS):
            for d in near:
                kv_core_got(slot, j, d).wait_recv()
    for e in range(1, side_x):
        o3_copy(e, False).wait_recv()

    low = lax.broadcasted_iota(jnp.int32, (BLOCK, 2 * HEAD), 1) < HEAD
    wide = 2 * BLOCK

    def attn_copy(t):
        return remote(attn.at[t], attn_got.at[t - 1], az_s.at[t - 1], az_r.at[t - 1], z_peer(t))

    part_copy = remote(part, part_got, pc_s, pc_r, core_peer)

    def out_copy(d):
        rows = pl.ds(pl.multiple_of(chip * BLOCK, BLOCK), BLOCK)
        return remote(out_send.at[d - 1], out.at[rows], oz_s.at[d - 1], oz_r.at[d - 1], z_peer(d))

    def out_got(d):
        rows = pl.ds(pl.multiple_of(behind(d) * BLOCK, BLOCK), BLOCK)
        return remote(out_send.at[d - 1], out.at[rows], oz_s.at[d - 1], oz_r.at[d - 1], z_peer(d))

    ones = low.astype(F32).astype(BF16)
    high = (1.0 - low.astype(F32)).astype(BF16)

    def attend(t, buf):
        i = ahead(t)
        for l in range(listed):
            block = lists[i, l]
            home = block // pool_blocks
            slot = jnp.where(home == region, 0, jnp.where(home == sibling[0], 1, 2))
            rows = slice(l * BLOCK, (l + 1) * BLOCK)
            pair = pool[slot * pool_blocks + lax.rem(block, pool_blocks)]
            kv_list[buf, 0, rows] = pair
            kv_list[buf, 1, rows] = (pair * high + ones) * jnp.full(pair.shape, keep[i, l], F32).astype(BF16)
        q = q_ext[i]
        top = jnp.full((wide, BLOCK), -jnp.inf, F32)
        for p in range(listed // 2):
            keys = kv_list[buf, 0, p * wide : (p + 1) * wide]
            s = lax.dot_general(q, keys, (((1,), (1,)), ((), ())), preferred_element_type=F32)
            scores[buf, :, p * wide : (p + 1) * wide] = s
            top = jnp.maximum(top, jnp.maximum(s[:, :BLOCK], s[:, BLOCK:]))
        top = jnp.max(top, axis=1, keepdims=True)
        mixed = jnp.zeros((wide, BLOCK), F32)
        for p in range(listed // 2):
            e = jnp.exp(scores[buf, :, p * wide : (p + 1) * wide] - top).astype(BF16)
            mixed += jnp.dot(e, kv_list[buf, 1, p * wide : (p + 1) * wide], preferred_element_type=F32)
        mixed = mixed / pltpu.roll(mixed, HEAD, 1)
        both = jnp.where(low, pltpu.roll(mixed[:BLOCK], HEAD, 1), mixed[BLOCK:])
        attn[t] = jnp.where(i < live[0], both, 0.0).astype(BF16)

    for n, t in enumerate((2, 1, 3, 0)):
        attend(t, n % 2)
        if t > 0:
            attn_copy(t).start()

    for d in far:
        attn_copy(d).wait_recv()
    heads = jnp.concatenate([attn[0]] + [attn_got[d - 1] for d in far], axis=1)

    def project(block):
        cols = pl.ds(pl.multiple_of(block * BLOCK, BLOCK), BLOCK)
        weight = jnp.concatenate(
            [ow[:, cols]] + [owz[pl.ds(block * 2, 2), d - 1].reshape(BLOCK, BLOCK) for d in far], axis=0
        )
        return jnp.dot(heads, weight, preferred_element_type=F32)

    for d in near:
        part[d] = project(ahead(d) * 2 + other).astype(BF16)
    part_copy.start()
    terms = [project(ahead(d) * 2 + core) for d in near]
    part_copy.wait_recv()
    for d in far:
        out_send[d - 1] = (terms[d] + part_got[d].astype(F32)).astype(BF16)
        out_copy(d).start()
    rows = pl.ds(pl.multiple_of(chip * BLOCK, BLOCK), BLOCK)
    out[rows, :] = (terms[0] + part_got[0].astype(F32)).astype(BF16)
    for d in far:
        out_got(d).wait_recv()

    part_copy.wait_send()
    for d in far:
        attn_copy(d).wait_send()
        out_copy(d).wait_send()
        o1_copy(d).wait_send()
    for e in range(1, side_y):
        o2_copy(e, True).wait_send()
    for e in range(1, side_x):
        o3_copy(e, True).wait_send()
    for j in range(CHUNKS):
        for d in near:
            mold_c_copy(j, d).wait_send()
            kv_sib(j, d).wait_send()
            kv_x(j, d).wait_send()
            for slot in range(3):
                kv_core(slot, j, d).wait_send()
        for d in far:
            mold_z_copy(j, d).wait_send()
        for t in range(3):
            kv_z_copy(j, t).wait_send()
    for d in far:
        w1_copy(d).wait_send()
        q_z_copy(d).wait_send()
        q_heads(d).wait_send()
    for e in range(1, side_x):
        w2_copy(e, True).wait_send()
    for e in range(1, side_y):
        w3_copy(e, True).wait_send()
    for d in near:
        q_core(d).wait_send()


def solution(mesh):
    regions, shards = mesh.shape["region"], mesh.shape["wshard"]
    chips = shards // 2

    def step(queries, mold, q_weight, k_weight, v_weight, o_weight, lists, live):
        rows_q, feats = queries.shape
        rows_m = mold.shape[0]
        width, kv_cols = k_weight.shape
        qblocks, listed = lists.shape
        pool_blocks = rows_m // BLOCK
        rows_j = rows_m // chips // CHUNKS
        half = rows_j // 2
        piece = half // BLOCK
        far = chips - 1
        columns = regions // 2
        dma = pltpu.SemaphoreType.DMA
        any_space = pl.BlockSpec(memory_space=pl.ANY)
        smem = pl.BlockSpec(memory_space=pltpu.SMEM)
        scratch = [
            pltpu.VMEM((rows_q, feats), BF16),
            pltpu.VMEM((shards, BLOCK, feats), BF16),
            pltpu.VMEM((chips, BLOCK, feats), BF16),
            pltpu.VMEM((far, BLOCK, feats), BF16),
            pltpu.VMEM(q_weight.shape, BF16),
            pltpu.VMEM((columns, far, width // columns, feats), BF16),
            pltpu.VMEM(k_weight.shape, BF16),
            pltpu.VMEM(v_weight.shape, BF16),
            pltpu.VMEM((width, 2 * kv_cols), BF16),
            pltpu.VMEM(o_weight.shape, BF16),
            pltpu.VMEM((rows_m, feats), BF16),
            pltpu.VMEM((CHUNKS, far, rows_j, feats), BF16),
            pltpu.VMEM((CHUNKS, chips, half, feats), BF16),
            pltpu.VMEM((CHUNKS, KV_HEADS, piece, BLOCK, 2 * HEAD), BF16),
            pltpu.VMEM((3 * pool_blocks, BLOCK, 2 * HEAD), BF16),
            pltpu.VMEM((2, 2, listed * BLOCK, 2 * HEAD), BF16),
            pltpu.VMEM((qblocks, 2 * BLOCK, 2 * HEAD), BF16),
            pltpu.VMEM((2, 2 * BLOCK, listed * BLOCK), F32),
            pltpu.SMEM((qblocks, listed), F32),
            pltpu.VMEM((columns, far, width // columns, feats), BF16),
            pltpu.VMEM((chips, BLOCK, 2 * HEAD), BF16),
            pltpu.VMEM((far, BLOCK, 2 * HEAD), BF16),
            pltpu.VMEM((chips, BLOCK, feats), BF16),
            pltpu.VMEM((chips, BLOCK, feats), BF16),
            pltpu.VMEM((far, BLOCK, feats), BF16),
            dma((6,)),
        ]
        for shape in (
            (CHUNKS, far),
            (CHUNKS, chips),
            (CHUNKS, 3),
            (3, CHUNKS, chips),
            (CHUNKS, chips),
            (CHUNKS, chips),
            (far,),
            (chips,),
            (far,),
            (far,),
            (3,),
            (regions // 8 - 1,),
            (far,),
            (regions // 8 - 1,),
            (3,),
            (far,),
            (),
            (far,),
        ):
            scratch += [dma(shape), dma(shape)]
        return pl.pallas_call(
            functools.partial(kernel, chips, regions),
            out_shape=jax.ShapeDtypeStruct((rows_q, feats), BF16),
            in_specs=[any_space] * 6 + [smem] * 2,
            out_specs=pl.BlockSpec(memory_space=pltpu.VMEM),
            scratch_shapes=scratch,
            compiler_params=pltpu.CompilerParams(
                collective_id=0, has_side_effects=True, vmem_limit_bytes=215 << 18
            ),
        )(queries, mold, q_weight, k_weight, v_weight, o_weight, lists, live)

    return jax.shard_map(
        step,
        mesh=mesh,
        in_specs=(
            P("region", "wshard"),
            P("region", "wshard"),
            P(None, "wshard"),
            P(),
            P(),
            P("wshard", None),
            P("region", None),
            P("region"),
        ),
        out_specs=P("region", "wshard"),
        check_vma=False,
    )
```

```python
import functools

import jax
import jax.numpy as jnp
from jax import lax
from jax.experimental import pallas as pl
from jax.experimental.pallas import tpu as pltpu
from jax.sharding import PartitionSpec as P

HEAD = 64
KV_HEADS = 4
BLOCK = 128
MESH = pl.DeviceIdType.MESH
CHUNKS = 2
F32, BF16 = jnp.float32, jnp.bfloat16


def kernel(
    chips,
    regions,
    queries,
    mold,
    q_weight,
    k_weight,
    v_weight,
    o_weight,
    lists,
    live,
    out,
    q_own,
    q_feats,
    q_rows,
    q_send,
    qw,
    qwz,
    kw,
    vw,
    wkv,
    ow,
    mold_own,
    mold_z,
    mold_c,
    kv_send,
    pool,
    kv_list,
    q_ext,
    scores,
    keep,
    owz,
    attn,
    attn_got,
    part,
    part_got,
    out_send,
    sem_local,
    mz_s,
    mz_r,
    mc_s,
    mc_r,
    kz_s,
    kz_r,
    kc_s,
    kc_r,
    ki_s,
    ki_r,
    kx_s,
    kx_r,
    qz_s,
    qz_r,
    qc_s,
    qc_r,
    qh_s,
    qh_r,
    w1_s,
    w1_r,
    w2_s,
    w2_r,
    w3_s,
    w3_r,
    o1_s,
    o1_r,
    o2_s,
    o2_r,
    o3_s,
    o3_r,
    az_s,
    az_r,
    pc_s,
    pc_r,
    oz_s,
    oz_r,
):
    region = lax.axis_index("region")
    shard = lax.axis_index("wshard")
    chip = shard // 2
    core = lax.rem(shard, 2)
    other = 1 - core
    odd = lax.rem(region, 2)
    qblocks, listed = lists.shape
    pool_blocks = pool.shape[0] // 3
    chip_blocks = pool_blocks // chips
    chip_rows = chip_blocks * BLOCK
    rows_j = chip_rows // CHUNKS
    half = rows_j // 2
    piece = half // BLOCK
    far = range(1, chips)
    near = range(chips)

    def ahead(d):
        return lax.rem(chip + d, chips)

    def behind(d):
        return lax.rem(chip + chips - d, chips)

    def z_peer(d):
        return (region, ahead(d) * 2 + core)

    core_peer = (region, chip * 2 + other)
    sibling = (region + 1 - 2 * odd, shard)
    x_to = (lax.rem(region + regions + 2 - 4 * odd, regions), shard)
    x_from = (lax.rem(region + regions - 2 + 4 * odd, regions), shard)
    column = region // 2
    side_x = 4
    side_y = regions // 2 // side_x
    at_x = lax.rem(column, side_x)
    at_y = column // side_x
    share = qwz.shape[2]
    step_s = 1 + 2 * odd
    offsets = (0, step_s, chips - step_s, 2)

    def x_peer(e):
        return ((at_y * side_x + lax.rem(at_x + e, side_x)) * 2 + odd, shard)

    def y_peer(e):
        return ((lax.rem(at_y + e, side_y) * side_x + at_x) * 2 + odd, shard)

    def sib_peer(d):
        return (sibling[0], ahead(d) * 2 + core)

    def remote(src, dst, send, recv, peer):
        return pltpu.make_async_remote_copy(
            src_ref=src, dst_ref=dst, send_sem=send, recv_sem=recv, device_id=peer, device_id_type=MESH
        )

    local = [
        pltpu.make_async_copy(k_weight, kw, sem_local.at[0]),
        pltpu.make_async_copy(v_weight, vw, sem_local.at[1]),
        pltpu.make_async_copy(q_weight, qw, sem_local.at[2]),
        pltpu.make_async_copy(o_weight, ow, sem_local.at[3]),
        pltpu.make_async_copy(queries, q_own, sem_local.at[4]),
        pltpu.make_async_copy(mold, mold_own, sem_local.at[5]),
    ]
    for copy in (local[5], local[2], local[3], local[0], local[1], local[4]):
        copy.start()

    barrier = pltpu.get_barrier_semaphore()
    partners = [z_peer(d) for d in far] + [core_peer, sibling, x_to, x_from]
    partners += [sib_peer(chips - step_s), sib_peer(2)]
    partners += [x_peer(e) for e in range(1, side_x)] + [y_peer(e) for e in range(1, side_y)]
    for peer in partners:
        pl.semaphore_signal(barrier, inc=1, device_id=peer, device_id_type=MESH)
    for copy in local:
        copy.wait()
    q_feats[shard] = q_own[pl.ds(pl.multiple_of(chip * BLOCK, BLOCK), BLOCK), :]
    for h in range(KV_HEADS):
        cols = slice(h * HEAD, (h + 1) * HEAD)
        wkv[:, h * 2 * HEAD : (h + 1) * 2 * HEAD] = jnp.concatenate([kw[:, cols], vw[:, cols]], axis=1)

    def mark(i, _):
        for l in range(listed):
            repeat = jnp.int32(0)
            for e in range(l):
                repeat = jnp.where(lists[i, e] == lists[i, l], jnp.int32(1), repeat)
            keep[i, l] = jnp.where(repeat == 1, F32(0.0), F32(1.0))
        return 0

    lax.fori_loop(0, qblocks, mark, 0)

    pl.semaphore_wait(barrier, len(partners))

    def w1_copy(d):
        rows = pl.ds(pl.multiple_of(column * share, share), share)
        return remote(qw.at[rows], qwz.at[column, d - 1], w1_s.at[d - 1], w1_r.at[d - 1], z_peer(d))

    def w2_copy(e, sent):
        spot = column if sent else at_y * side_x + lax.rem(at_x + side_x - e, side_x)
        return remote(qwz.at[column], qwz.at[spot], w2_s.at[e - 1], w2_r.at[e - 1], x_peer(e))

    def w3_copy(e, sent):
        mine = pl.ds(at_y * side_x, side_x)
        spot = mine if sent else pl.ds(lax.rem(at_y + side_y - e, side_y) * side_x, side_x)
        return remote(qwz.at[mine], qwz.at[spot], w3_s.at[e - 1], w3_r.at[e - 1], y_peer(e))

    column_o = at_x * side_y + at_y

    def o1_copy(d):
        rows = pl.ds(pl.multiple_of(lax.rem(column_o, 2) * share, share), share)
        cols = pl.ds(pl.multiple_of(column_o // 2 * BLOCK, BLOCK), BLOCK)
        return remote(ow.at[rows, cols], owz.at[column_o, d - 1], o1_s.at[d - 1], o1_r.at[d - 1], z_peer(d))

    def o2_copy(e, sent):
        spot = column_o if sent else at_x * side_y + lax.rem(at_y + side_y - e, side_y)
        return remote(owz.at[column_o], owz.at[spot], o2_s.at[e - 1], o2_r.at[e - 1], y_peer(e))

    def o3_copy(e, sent):
        mine = pl.ds(at_x * side_y, side_y)
        spot = mine if sent else pl.ds(lax.rem(at_x + side_x - e, side_x) * side_y, side_y)
        return remote(owz.at[mine], owz.at[spot], o3_s.at[e - 1], o3_r.at[e - 1], x_peer(e))

    for d in far:
        w1_copy(d).start()
    for d in far:
        o1_copy(d).start()

    def mold_z_copy(j, d):
        row = pl.multiple_of(ahead(d) * chip_rows + j * rows_j, BLOCK)
        return remote(
            mold_own.at[pl.ds(row, rows_j)], mold_z.at[j, d - 1], mz_s.at[j, d - 1], mz_r.at[j, d - 1], z_peer(d)
        )

    for j in range(CHUNKS):
        for d in (2, 1, 3):
            mold_z_copy(j, d).start()

    def mold_src(j, d, side):
        rows = pl.ds(pl.multiple_of(side * half, BLOCK), half)
        if d == 0:
            return mold_own.at[pl.ds(pl.multiple_of(chip * chip_rows + j * rows_j + side * half, BLOCK), half)]
        return mold_z.at[j, d - 1, rows]

    def mold_c_copy(j, d):
        return remote(mold_src(j, d, other), mold_c.at[j, d], mc_s.at[j, d], mc_r.at[j, d], core_peer)

    for j in range(CHUNKS):
        mold_c_copy(j, 0).start()

    def at_piece(slot, j, off, side):
        return pl.ds(slot * pool_blocks + behind(off) * chip_blocks + (j * 2 + side) * piece, piece)

    z_routes = ((step_s, 0), (chips - step_s, 1), (2, 1))
    z_arrivals = ((0, 1), (1, 1), (1, 3))

    def kv_z_copy(j, t):
        d, slot = z_routes[t]
        peer = sib_peer(d) if slot else z_peer(d)
        spot = at_piece(slot, j, 0, core)
        return remote(kv_send.at[j, ahead(d)], pool.at[spot], kz_s.at[j, t], kz_r.at[j, t], peer)

    def kv_z_got(j, t):
        slot, at = z_arrivals[t]
        spot = at_piece(slot, j, offsets[at], core)
        return remote(kv_send.at[j, 0], pool.at[spot], kz_s.at[j, t], kz_r.at[j, t], sibling)

    def kv_core(slot, j, t):
        spot = at_piece(slot, j, offsets[t], core)
        return remote(pool.at[spot], pool.at[spot], kc_s.at[slot, j, t], kc_r.at[slot, j, t], core_peer)

    def kv_core_got(slot, j, t):
        spot = at_piece(slot, j, offsets[t], other)
        return remote(pool.at[spot], pool.at[spot], kc_s.at[slot, j, t], kc_r.at[slot, j, t], core_peer)

    sib_sent = ((0, 0), (0, 1), (1, 1), (1, 3))
    sib_arrivals = ((1, 0), (1, 2), (0, 2), (0, 3))

    def kv_sib(j, t):
        slot, at = sib_sent[t]
        src = at_piece(slot, j, offsets[at], core)
        dst = at_piece(1 - slot, j, offsets[at], core)
        return remote(pool.at[src], pool.at[dst], ki_s.at[j, t], ki_r.at[j, t], sibling)

    def kv_sib_got(j, t):
        slot, at = sib_arrivals[t]
        spot = at_piece(slot, j, offsets[at], core)
        return remote(pool.at[spot], pool.at[spot], ki_s.at[j, t], ki_r.at[j, t], sibling)

    def kv_x(j, t):
        return remote(
            pool.at[at_piece(1, j, offsets[t], core)],
            pool.at[at_piece(2, j, offsets[t], core)],
            kx_s.at[j, t],
            kx_r.at[j, t],
            x_to,
        )

    def q_z_copy(d):
        rows = pl.ds(pl.multiple_of(ahead(d) * BLOCK, BLOCK), BLOCK)
        return remote(q_own.at[rows], q_feats.at[shard], qz_s.at[d - 1], qz_r.at[d - 1], z_peer(d))

    def q_z_got(d):
        return remote(q_send.at[0], q_feats.at[behind(d) * 2 + core], qz_s.at[d - 1], qz_r.at[d - 1], z_peer(d))

    def q_core(d):
        spot = q_feats.at[behind(d) * 2 + core]
        return remote(spot, spot, qc_s.at[d], qc_r.at[d], core_peer)

    def q_core_got(d):
        spot = q_feats.at[behind(d) * 2 + other]
        return remote(spot, spot, qc_s.at[d], qc_r.at[d], core_peer)

    def q_heads(d):
        return remote(q_send.at[d - 1], q_rows.at[chip], qh_s.at[d - 1], qh_r.at[d - 1], z_peer(d))

    def q_heads_got(d):
        return remote(q_send.at[d - 1], q_rows.at[behind(d)], qh_s.at[d - 1], qh_r.at[d - 1], z_peer(d))

    q_core(0).start()
    for d in far:
        q_z_copy(d).start()
    for d in far:
        w1_copy(d).wait_recv()
    for e in range(1, side_x):
        w2_copy(e, True).start()
    for d in far:
        o1_copy(d).wait_recv()
    for e in range(1, side_y):
        o2_copy(e, True).start()
    for e in range(1, side_x):
        w2_copy(e, False).wait_recv()
    for e in range(1, side_y):
        w3_copy(e, True).start()

    for j in range(CHUNKS):
        for d in (2, 1, 3):
            mold_z_copy(j, d).wait_recv()
            mold_c_copy(j, d).start()
        total = jnp.zeros((half, wkv.shape[1]), F32)
        for d in near:
            depth = 2 * BLOCK
            base = pl.multiple_of(behind(d) * depth, depth)
            mine = wkv[pl.ds(pl.multiple_of(base + core * BLOCK, BLOCK), BLOCK), :]
            total += jnp.dot(mold_src(j, d, core)[...], mine, preferred_element_type=F32)
            mold_c_copy(j, d).wait_recv()
            theirs = wkv[pl.ds(pl.multiple_of(base + other * BLOCK, BLOCK), BLOCK), :]
            total += jnp.dot(mold_c[j, d], theirs, preferred_element_type=F32)
        pairs = total.astype(BF16)
        for h in range(KV_HEADS):
            kv_send[j, h] = pairs[:, h * BLOCK : (h + 1) * BLOCK].reshape(piece, BLOCK, BLOCK)
        pool[at_piece(0, j, 0, core)] = kv_send[j, chip]
        for t in range(3):
            kv_z_copy(j, t).start()
        kv_sib(j, 0).start()
        kv_core(0, j, 0).start()
        if j == 0:
            for e in range(1, side_y):
                o2_copy(e, False).wait_recv()
            for e in range(1, side_x):
                o3_copy(e, True).start()

    def forward(j):
        for t in range(3):
            kv_z_got(j, t).wait_recv()
            slot, at = z_arrivals[t]
            kv_sib(j, t + 1).start()
            if slot == 1:
                kv_x(j, at).start()
            kv_core(slot, j, at).start()

    forward(0)

    for d in far:
        q_z_got(d).wait_recv()
        q_core(d).start()
    for e in range(1, side_y):
        w3_copy(e, False).wait_recv()
    for d in near:
        q_core_got(d).wait_recv()
    feats = jnp.concatenate([q_feats[f] for f in range(q_feats.shape[0])], axis=1)

    def project_q(weight):
        value = jnp.dot(feats, weight, preferred_element_type=F32).astype(BF16)
        return (value.astype(F32) * HEAD**-0.5).astype(BF16)

    for d in far:
        q_send[d - 1] = project_q(qwz[:, chips - d - 1].reshape(qw.shape))
        q_heads(d).start()
    q_rows[chip] = project_q(qw[...])

    for j in range(1, CHUNKS):
        forward(j)
    for j in range(CHUNKS):
        for t in range(4):
            kv_sib_got(j, t).wait_recv()
            slot, at = sib_arrivals[t]
            if slot == 1:
                kv_x(j, at).start()
            kv_core(slot, j, at).start()

    lane = lax.broadcasted_iota(jnp.int32, (BLOCK, 2 * HEAD), 1)
    for d in far:
        q_heads_got(d).wait_recv()
    for i in range(qblocks):
        value = q_rows[i].astype(F32)
        q_ext[i, :BLOCK] = jnp.where(lane < HEAD, value, 0.0).astype(BF16)
        q_ext[i, BLOCK:] = jnp.where(lane < HEAD, pltpu.roll(value, HEAD, 1), 0.0).astype(BF16)

    for j in range(CHUNKS):
        for t in (1, 3, 0, 2):
            kv_x(j, t).wait_recv()
            kv_core(2, j, t).start()

    for slot in range(3):
        for j in range(CHUNKS):
            for d in near:
                kv_core_got(slot, j, d).wait_recv()
    for e in range(1, side_x):
        o3_copy(e, False).wait_recv()

    low = lax.broadcasted_iota(jnp.int32, (BLOCK, 2 * HEAD), 1) < HEAD
    wide = 2 * BLOCK

    def attn_copy(t):
        return remote(attn.at[t], attn_got.at[t - 1], az_s.at[t - 1], az_r.at[t - 1], z_peer(t))

    part_copy = remote(part, part_got, pc_s, pc_r, core_peer)

    def out_copy(d):
        rows = pl.ds(pl.multiple_of(chip * BLOCK, BLOCK), BLOCK)
        return remote(out_send.at[d - 1], out.at[rows], oz_s.at[d - 1], oz_r.at[d - 1], z_peer(d))

    def out_got(d):
        rows = pl.ds(pl.multiple_of(behind(d) * BLOCK, BLOCK), BLOCK)
        return remote(out_send.at[d - 1], out.at[rows], oz_s.at[d - 1], oz_r.at[d - 1], z_peer(d))

    ones = low.astype(F32).astype(BF16)
    high = (1.0 - low.astype(F32)).astype(BF16)

    def attend(t, buf):
        i = ahead(t)
        for l in range(listed):
            block = lists[i, l]
            home = block // pool_blocks
            slot = jnp.where(home == region, 0, jnp.where(home == sibling[0], 1, 2))
            rows = slice(l * BLOCK, (l + 1) * BLOCK)
            pair = pool[slot * pool_blocks + lax.rem(block, pool_blocks)]
            kv_list[buf, 0, rows] = pair
            kv_list[buf, 1, rows] = (pair * high + ones) * jnp.full(pair.shape, keep[i, l], F32).astype(BF16)
        q = q_ext[i]
        top = jnp.full((wide, BLOCK), -jnp.inf, F32)
        for p in range(listed // 2):
            keys = kv_list[buf, 0, p * wide : (p + 1) * wide]
            s = lax.dot_general(q, keys, (((1,), (1,)), ((), ())), preferred_element_type=F32)
            scores[buf, :, p * wide : (p + 1) * wide] = s
            top = jnp.maximum(top, jnp.maximum(s[:, :BLOCK], s[:, BLOCK:]))
        top = jnp.max(top, axis=1, keepdims=True)
        mixed = jnp.zeros((wide, BLOCK), F32)
        for p in range(listed // 2):
            e = jnp.exp(scores[buf, :, p * wide : (p + 1) * wide] - top).astype(BF16)
            mixed += jnp.dot(e, kv_list[buf, 1, p * wide : (p + 1) * wide], preferred_element_type=F32)
        mixed = mixed / pltpu.roll(mixed, HEAD, 1)
        both = jnp.where(low, pltpu.roll(mixed[:BLOCK], HEAD, 1), mixed[BLOCK:])
        attn[t] = jnp.where(i < live[0], both, 0.0).astype(BF16)

    for n, t in enumerate((2, 1, 3, 0)):
        attend(t, n % 2)
        if t > 0:
            attn_copy(t).start()

    for d in far:
        attn_copy(d).wait_recv()
    heads = jnp.concatenate([attn[0]] + [attn_got[d - 1] for d in far], axis=1)

    def project(block):
        cols = pl.ds(pl.multiple_of(block * BLOCK, BLOCK), BLOCK)
        weight = jnp.concatenate(
            [ow[:, cols]] + [owz[pl.ds(block * 2, 2), d - 1].reshape(BLOCK, BLOCK) for d in far], axis=0
        )
        return jnp.dot(heads, weight, preferred_element_type=F32)

    for d in near:
        part[d] = project(ahead(d) * 2 + other).astype(BF16)
    part_copy.start()
    terms = [project(ahead(d) * 2 + core) for d in near]
    part_copy.wait_recv()
    for d in far:
        out_send[d - 1] = (terms[d] + part_got[d].astype(F32)).astype(BF16)
        out_copy(d).start()
    rows = pl.ds(pl.multiple_of(chip * BLOCK, BLOCK), BLOCK)
    out[rows, :] = (terms[0] + part_got[0].astype(F32)).astype(BF16)
    for d in far:
        out_got(d).wait_recv()

    part_copy.wait_send()
    for d in far:
        attn_copy(d).wait_send()
        out_copy(d).wait_send()
        o1_copy(d).wait_send()
    for e in range(1, side_y):
        o2_copy(e, True).wait_send()
    for e in range(1, side_x):
        o3_copy(e, True).wait_send()
    for j in range(CHUNKS):
        for d in near:
            mold_c_copy(j, d).wait_send()
            kv_sib(j, d).wait_send()
            kv_x(j, d).wait_send()
            for slot in range(3):
                kv_core(slot, j, d).wait_send()
        for d in far:
            mold_z_copy(j, d).wait_send()
        for t in range(3):
            kv_z_copy(j, t).wait_send()
    for d in far:
        w1_copy(d).wait_send()
        q_z_copy(d).wait_send()
        q_heads(d).wait_send()
    for e in range(1, side_x):
        w2_copy(e, True).wait_send()
    for e in range(1, side_y):
        w3_copy(e, True).wait_send()
    for d in near:
        q_core(d).wait_send()


def solution(mesh):
    regions, shards = mesh.shape["region"], mesh.shape["wshard"]
    chips = shards // 2

    def step(queries, mold, q_weight, k_weight, v_weight, o_weight, lists, live):
        rows_q, feats = queries.shape
        rows_m = mold.shape[0]
        width, kv_cols = k_weight.shape
        qblocks, listed = lists.shape
        pool_blocks = rows_m // BLOCK
        rows_j = rows_m // chips // CHUNKS
        half = rows_j // 2
        piece = half // BLOCK
        far = chips - 1
        columns = regions // 2
        dma = pltpu.SemaphoreType.DMA
        any_space = pl.BlockSpec(memory_space=pl.ANY)
        smem = pl.BlockSpec(memory_space=pltpu.SMEM)
        scratch = [
            pltpu.VMEM((rows_q, feats), BF16),
            pltpu.VMEM((shards, BLOCK, feats), BF16),
            pltpu.VMEM((chips, BLOCK, feats), BF16),
            pltpu.VMEM((far, BLOCK, feats), BF16),
            pltpu.VMEM(q_weight.shape, BF16),
            pltpu.VMEM((columns, far, width // columns, feats), BF16),
            pltpu.VMEM(k_weight.shape, BF16),
            pltpu.VMEM(v_weight.shape, BF16),
            pltpu.VMEM((width, 2 * kv_cols), BF16),
            pltpu.VMEM(o_weight.shape, BF16),
            pltpu.VMEM((rows_m, feats), BF16),
            pltpu.VMEM((CHUNKS, far, rows_j, feats), BF16),
            pltpu.VMEM((CHUNKS, chips, half, feats), BF16),
            pltpu.VMEM((CHUNKS, KV_HEADS, piece, BLOCK, 2 * HEAD), BF16),
            pltpu.VMEM((3 * pool_blocks, BLOCK, 2 * HEAD), BF16),
            pltpu.VMEM((2, 2, listed * BLOCK, 2 * HEAD), BF16),
            pltpu.VMEM((qblocks, 2 * BLOCK, 2 * HEAD), BF16),
            pltpu.VMEM((2, 2 * BLOCK, listed * BLOCK), F32),
            pltpu.SMEM((qblocks, listed), F32),
            pltpu.VMEM((columns, far, width // columns, feats), BF16),
            pltpu.VMEM((chips, BLOCK, 2 * HEAD), BF16),
            pltpu.VMEM((far, BLOCK, 2 * HEAD), BF16),
            pltpu.VMEM((chips, BLOCK, feats), BF16),
            pltpu.VMEM((chips, BLOCK, feats), BF16),
            pltpu.VMEM((far, BLOCK, feats), BF16),
            dma((6,)),
        ]
        for shape in (
            (CHUNKS, far),
            (CHUNKS, chips),
            (CHUNKS, 3),
            (3, CHUNKS, chips),
            (CHUNKS, chips),
            (CHUNKS, chips),
            (far,),
            (chips,),
            (far,),
            (far,),
            (3,),
            (regions // 8 - 1,),
            (far,),
            (regions // 8 - 1,),
            (3,),
            (far,),
            (),
            (far,),
        ):
            scratch += [dma(shape), dma(shape)]
        return pl.pallas_call(
            functools.partial(kernel, chips, regions),
            out_shape=jax.ShapeDtypeStruct((rows_q, feats), BF16),
            in_specs=[any_space] * 6 + [smem] * 2,
            out_specs=pl.BlockSpec(memory_space=pltpu.VMEM),
            scratch_shapes=scratch,
            compiler_params=pltpu.CompilerParams(
                collective_id=0, has_side_effects=True, vmem_limit_bytes=215 << 18
            ),
        )(queries, mold, q_weight, k_weight, v_weight, o_weight, lists, live)

    return jax.shard_map(
        step,
        mesh=mesh,
        in_specs=(
            P("region", "wshard"),
            P("region", "wshard"),
            P(None, "wshard"),
            P(),
            P(),
            P("wshard", None),
            P("region", None),
            P("region"),
        ),
        out_specs=P("region", "wshard"),
        check_vma=False,
    )
```

```python
import functools

import jax
import jax.numpy as jnp
from jax import lax
from jax.experimental import pallas as pl
from jax.experimental.pallas import tpu as pltpu
from jax.sharding import PartitionSpec as P

HEAD = 64
KV_HEADS = 4
BLOCK = 128
MESH = pl.DeviceIdType.MESH
CHUNKS = 2
F32, BF16 = jnp.float32, jnp.bfloat16


def kernel(
    chips,
    regions,
    queries,
    mold,
    q_weight,
    k_weight,
    v_weight,
    o_weight,
    lists,
    live,
    out,
    q_own,
    q_feats,
    q_rows,
    q_send,
    qw,
    qwz,
    kw,
    vw,
    wkv,
    ow,
    mold_own,
    mold_z,
    mold_c,
    kv_send,
    pool,
    kv_list,
    q_ext,
    scores,
    keep,
    owz,
    attn,
    attn_got,
    part,
    part_got,
    out_send,
    sem_local,
    mz_s,
    mz_r,
    mc_s,
    mc_r,
    kz_s,
    kz_r,
    kc_s,
    kc_r,
    ki_s,
    ki_r,
    kx_s,
    kx_r,
    qz_s,
    qz_r,
    qc_s,
    qc_r,
    qh_s,
    qh_r,
    w1_s,
    w1_r,
    w2_s,
    w2_r,
    w3_s,
    w3_r,
    o1_s,
    o1_r,
    o2_s,
    o2_r,
    o3_s,
    o3_r,
    az_s,
    az_r,
    pc_s,
    pc_r,
    oz_s,
    oz_r,
):
    region = lax.axis_index("region")
    shard = lax.axis_index("wshard")
    chip = shard // 2
    core = lax.rem(shard, 2)
    other = 1 - core
    odd = lax.rem(region, 2)
    qblocks, listed = lists.shape
    pool_blocks = pool.shape[0] // 3
    chip_blocks = pool_blocks // chips
    chip_rows = chip_blocks * BLOCK
    rows_j = chip_rows // CHUNKS
    half = rows_j // 2
    piece = half // BLOCK
    far = range(1, chips)
    near = range(chips)

    def ahead(d):
        return lax.rem(chip + d, chips)

    def behind(d):
        return lax.rem(chip + chips - d, chips)

    def z_peer(d):
        return (region, ahead(d) * 2 + core)

    core_peer = (region, chip * 2 + other)
    sibling = (region + 1 - 2 * odd, shard)
    x_to = (lax.rem(region + regions + 2 - 4 * odd, regions), shard)
    x_from = (lax.rem(region + regions - 2 + 4 * odd, regions), shard)
    column = region // 2
    side_x = 4
    side_y = regions // 2 // side_x
    at_x = lax.rem(column, side_x)
    at_y = column // side_x
    share = qwz.shape[2]
    step_s = 1 + 2 * odd
    offsets = (0, step_s, chips - step_s, 2)

    def x_peer(e):
        return ((at_y * side_x + lax.rem(at_x + e, side_x)) * 2 + odd, shard)

    def y_peer(e):
        return ((lax.rem(at_y + e, side_y) * side_x + at_x) * 2 + odd, shard)

    def sib_peer(d):
        return (sibling[0], ahead(d) * 2 + core)

    def remote(src, dst, send, recv, peer):
        return pltpu.make_async_remote_copy(
            src_ref=src, dst_ref=dst, send_sem=send, recv_sem=recv, device_id=peer, device_id_type=MESH
        )

    local = [
        pltpu.make_async_copy(k_weight, kw, sem_local.at[0]),
        pltpu.make_async_copy(v_weight, vw, sem_local.at[1]),
        pltpu.make_async_copy(q_weight, qw, sem_local.at[2]),
        pltpu.make_async_copy(o_weight, ow, sem_local.at[3]),
        pltpu.make_async_copy(queries, q_own, sem_local.at[4]),
        pltpu.make_async_copy(mold, mold_own, sem_local.at[5]),
    ]
    for copy in (local[5], local[2], local[3], local[0], local[1], local[4]):
        copy.start()

    barrier = pltpu.get_barrier_semaphore()
    partners = [z_peer(d) for d in far] + [core_peer, sibling, x_to, x_from]
    partners += [sib_peer(chips - step_s), sib_peer(2)]
    partners += [x_peer(e) for e in range(1, side_x)] + [y_peer(e) for e in range(1, side_y)]
    for peer in partners:
        pl.semaphore_signal(barrier, inc=1, device_id=peer, device_id_type=MESH)
    for copy in local:
        copy.wait()
    q_feats[shard] = q_own[pl.ds(pl.multiple_of(chip * BLOCK, BLOCK), BLOCK), :]
    for h in range(KV_HEADS):
        cols = slice(h * HEAD, (h + 1) * HEAD)
        wkv[:, h * 2 * HEAD : (h + 1) * 2 * HEAD] = jnp.concatenate([kw[:, cols], vw[:, cols]], axis=1)

    def mark(i, _):
        for l in range(listed):
            repeat = jnp.int32(0)
            for e in range(l):
                repeat = jnp.where(lists[i, e] == lists[i, l], jnp.int32(1), repeat)
            keep[i, l] = jnp.where(repeat == 1, F32(0.0), F32(1.0))
        return 0

    lax.fori_loop(0, qblocks, mark, 0)

    pl.semaphore_wait(barrier, len(partners))

    def w1_copy(d):
        rows = pl.ds(pl.multiple_of(column * share, share), share)
        return remote(qw.at[rows], qwz.at[column, d - 1], w1_s.at[d - 1], w1_r.at[d - 1], z_peer(d))

    def w2_copy(e, sent):
        spot = column if sent else at_y * side_x + lax.rem(at_x + side_x - e, side_x)
        return remote(qwz.at[column], qwz.at[spot], w2_s.at[e - 1], w2_r.at[e - 1], x_peer(e))

    def w3_copy(e, sent):
        mine = pl.ds(at_y * side_x, side_x)
        spot = mine if sent else pl.ds(lax.rem(at_y + side_y - e, side_y) * side_x, side_x)
        return remote(qwz.at[mine], qwz.at[spot], w3_s.at[e - 1], w3_r.at[e - 1], y_peer(e))

    column_o = at_x * side_y + at_y

    def o1_copy(d):
        rows = pl.ds(pl.multiple_of(lax.rem(column_o, 2) * share, share), share)
        cols = pl.ds(pl.multiple_of(column_o // 2 * BLOCK, BLOCK), BLOCK)
        return remote(ow.at[rows, cols], owz.at[column_o, d - 1], o1_s.at[d - 1], o1_r.at[d - 1], z_peer(d))

    def o2_copy(e, sent):
        spot = column_o if sent else at_x * side_y + lax.rem(at_y + side_y - e, side_y)
        return remote(owz.at[column_o], owz.at[spot], o2_s.at[e - 1], o2_r.at[e - 1], y_peer(e))

    def o3_copy(e, sent):
        mine = pl.ds(at_x * side_y, side_y)
        spot = mine if sent else pl.ds(lax.rem(at_x + side_x - e, side_x) * side_y, side_y)
        return remote(owz.at[mine], owz.at[spot], o3_s.at[e - 1], o3_r.at[e - 1], x_peer(e))

    for d in far:
        w1_copy(d).start()
    for d in far:
        o1_copy(d).start()

    def mold_z_copy(j, d):
        row = pl.multiple_of(ahead(d) * chip_rows + j * rows_j, BLOCK)
        return remote(
            mold_own.at[pl.ds(row, rows_j)], mold_z.at[j, d - 1], mz_s.at[j, d - 1], mz_r.at[j, d - 1], z_peer(d)
        )

    for j in range(CHUNKS):
        for d in (2, 1, 3):
            mold_z_copy(j, d).start()

    def mold_src(j, d, side):
        rows = pl.ds(pl.multiple_of(side * half, BLOCK), half)
        if d == 0:
            return mold_own.at[pl.ds(pl.multiple_of(chip * chip_rows + j * rows_j + side * half, BLOCK), half)]
        return mold_z.at[j, d - 1, rows]

    def mold_c_copy(j, d):
        return remote(mold_src(j, d, other), mold_c.at[j, d], mc_s.at[j, d], mc_r.at[j, d], core_peer)

    for j in range(CHUNKS):
        mold_c_copy(j, 0).start()

    def at_piece(slot, j, off, side):
        return pl.ds(slot * pool_blocks + behind(off) * chip_blocks + (j * 2 + side) * piece, piece)

    z_routes = ((step_s, 0), (chips - step_s, 1), (2, 1))
    z_arrivals = ((0, 1), (1, 1), (1, 3))

    def kv_z_copy(j, t):
        d, slot = z_routes[t]
        peer = sib_peer(d) if slot else z_peer(d)
        spot = at_piece(slot, j, 0, core)
        return remote(kv_send.at[j, ahead(d)], pool.at[spot], kz_s.at[j, t], kz_r.at[j, t], peer)

    def kv_z_got(j, t):
        slot, at = z_arrivals[t]
        spot = at_piece(slot, j, offsets[at], core)
        return remote(kv_send.at[j, 0], pool.at[spot], kz_s.at[j, t], kz_r.at[j, t], sibling)

    def kv_core(slot, j, t):
        spot = at_piece(slot, j, offsets[t], core)
        return remote(pool.at[spot], pool.at[spot], kc_s.at[slot, j, t], kc_r.at[slot, j, t], core_peer)

    def kv_core_got(slot, j, t):
        spot = at_piece(slot, j, offsets[t], other)
        return remote(pool.at[spot], pool.at[spot], kc_s.at[slot, j, t], kc_r.at[slot, j, t], core_peer)

    sib_sent = ((0, 0), (0, 1), (1, 1), (1, 3))
    sib_arrivals = ((1, 0), (1, 2), (0, 2), (0, 3))

    def kv_sib(j, t):
        slot, at = sib_sent[t]
        src = at_piece(slot, j, offsets[at], core)
        dst = at_piece(1 - slot, j, offsets[at], core)
        return remote(pool.at[src], pool.at[dst], ki_s.at[j, t], ki_r.at[j, t], sibling)

    def kv_sib_got(j, t):
        slot, at = sib_arrivals[t]
        spot = at_piece(slot, j, offsets[at], core)
        return remote(pool.at[spot], pool.at[spot], ki_s.at[j, t], ki_r.at[j, t], sibling)

    def kv_x(j, t):
        return remote(
            pool.at[at_piece(1, j, offsets[t], core)],
            pool.at[at_piece(2, j, offsets[t], core)],
            kx_s.at[j, t],
            kx_r.at[j, t],
            x_to,
        )

    def q_z_copy(d):
        rows = pl.ds(pl.multiple_of(ahead(d) * BLOCK, BLOCK), BLOCK)
        return remote(q_own.at[rows], q_feats.at[shard], qz_s.at[d - 1], qz_r.at[d - 1], z_peer(d))

    def q_z_got(d):
        return remote(q_send.at[0], q_feats.at[behind(d) * 2 + core], qz_s.at[d - 1], qz_r.at[d - 1], z_peer(d))

    def q_core(d):
        spot = q_feats.at[behind(d) * 2 + core]
        return remote(spot, spot, qc_s.at[d], qc_r.at[d], core_peer)

    def q_core_got(d):
        spot = q_feats.at[behind(d) * 2 + other]
        return remote(spot, spot, qc_s.at[d], qc_r.at[d], core_peer)

    def q_heads(d):
        return remote(q_send.at[d - 1], q_rows.at[chip], qh_s.at[d - 1], qh_r.at[d - 1], z_peer(d))

    def q_heads_got(d):
        return remote(q_send.at[d - 1], q_rows.at[behind(d)], qh_s.at[d - 1], qh_r.at[d - 1], z_peer(d))

    q_core(0).start()
    for d in far:
        q_z_copy(d).start()
    for d in far:
        w1_copy(d).wait_recv()
    for e in range(1, side_x):
        w2_copy(e, True).start()
    for d in far:
        o1_copy(d).wait_recv()
    for e in range(1, side_y):
        o2_copy(e, True).start()
    for e in range(1, side_x):
        w2_copy(e, False).wait_recv()
    for e in range(1, side_y):
        w3_copy(e, True).start()

    for j in range(CHUNKS):
        for d in (2, 1, 3):
            mold_z_copy(j, d).wait_recv()
            mold_c_copy(j, d).start()
        total = jnp.zeros((half, wkv.shape[1]), F32)
        for d in near:
            depth = 2 * BLOCK
            base = pl.multiple_of(behind(d) * depth, depth)
            mine = wkv[pl.ds(pl.multiple_of(base + core * BLOCK, BLOCK), BLOCK), :]
            total += jnp.dot(mold_src(j, d, core)[...], mine, preferred_element_type=F32)
            mold_c_copy(j, d).wait_recv()
            theirs = wkv[pl.ds(pl.multiple_of(base + other * BLOCK, BLOCK), BLOCK), :]
            total += jnp.dot(mold_c[j, d], theirs, preferred_element_type=F32)
        pairs = total.astype(BF16)
        for h in range(KV_HEADS):
            kv_send[j, h] = pairs[:, h * BLOCK : (h + 1) * BLOCK].reshape(piece, BLOCK, BLOCK)
        pool[at_piece(0, j, 0, core)] = kv_send[j, chip]
        for t in range(3):
            kv_z_copy(j, t).start()
        kv_sib(j, 0).start()
        kv_core(0, j, 0).start()
        if j == 0:
            for e in range(1, side_y):
                o2_copy(e, False).wait_recv()
            for e in range(1, side_x):
                o3_copy(e, True).start()

    def forward(j):
        for t in range(3):
            kv_z_got(j, t).wait_recv()
            slot, at = z_arrivals[t]
            kv_sib(j, t + 1).start()
            if slot == 1:
                kv_x(j, at).start()
            kv_core(slot, j, at).start()

    for d in far:
        q_z_got(d).wait_recv()
        q_core(d).start()
    forward(0)

    for e in range(1, side_y):
        w3_copy(e, False).wait_recv()
    for d in near:
        q_core_got(d).wait_recv()
    feats = jnp.concatenate([q_feats[f] for f in range(q_feats.shape[0])], axis=1)

    def project_q(weight):
        value = jnp.dot(feats, weight, preferred_element_type=F32).astype(BF16)
        return (value.astype(F32) * HEAD**-0.5).astype(BF16)

    for d in far:
        q_send[d - 1] = project_q(qwz[:, chips - d - 1].reshape(qw.shape))
        q_heads(d).start()
    q_rows[chip] = project_q(qw[...])

    for j in range(1, CHUNKS):
        forward(j)
    for j in range(CHUNKS):
        for t in range(4):
            kv_sib_got(j, t).wait_recv()
            slot, at = sib_arrivals[t]
            if slot == 1:
                kv_x(j, at).start()
            kv_core(slot, j, at).start()

    lane = lax.broadcasted_iota(jnp.int32, (BLOCK, 2 * HEAD), 1)
    for d in far:
        q_heads_got(d).wait_recv()
    for i in range(qblocks):
        value = q_rows[i].astype(F32)
        q_ext[i, :BLOCK] = jnp.where(lane < HEAD, value, 0.0).astype(BF16)
        q_ext[i, BLOCK:] = jnp.where(lane < HEAD, pltpu.roll(value, HEAD, 1), 0.0).astype(BF16)

    for j in range(CHUNKS):
        for t in (1, 3, 0, 2):
            kv_x(j, t).wait_recv()
            kv_core(2, j, t).start()

    for slot in range(3):
        for j in range(CHUNKS):
            for d in near:
                kv_core_got(slot, j, d).wait_recv()
    for e in range(1, side_x):
        o3_copy(e, False).wait_recv()

    low = lax.broadcasted_iota(jnp.int32, (BLOCK, 2 * HEAD), 1) < HEAD
    wide = 2 * BLOCK

    def attn_copy(t):
        return remote(attn.at[t], attn_got.at[t - 1], az_s.at[t - 1], az_r.at[t - 1], z_peer(t))

    part_copy = remote(part, part_got, pc_s, pc_r, core_peer)

    def out_copy(d):
        rows = pl.ds(pl.multiple_of(chip * BLOCK, BLOCK), BLOCK)
        return remote(out_send.at[d - 1], out.at[rows], oz_s.at[d - 1], oz_r.at[d - 1], z_peer(d))

    def out_got(d):
        rows = pl.ds(pl.multiple_of(behind(d) * BLOCK, BLOCK), BLOCK)
        return remote(out_send.at[d - 1], out.at[rows], oz_s.at[d - 1], oz_r.at[d - 1], z_peer(d))

    ones = low.astype(F32).astype(BF16)
    high = (1.0 - low.astype(F32)).astype(BF16)

    def attend(t, buf):
        i = ahead(t)
        for l in range(listed):
            block = lists[i, l]
            home = block // pool_blocks
            slot = jnp.where(home == region, 0, jnp.where(home == sibling[0], 1, 2))
            rows = slice(l * BLOCK, (l + 1) * BLOCK)
            pair = pool[slot * pool_blocks + lax.rem(block, pool_blocks)]
            kv_list[buf, 0, rows] = pair
            kv_list[buf, 1, rows] = (pair * high + ones) * jnp.full(pair.shape, keep[i, l], F32).astype(BF16)
        q = q_ext[i]
        top = jnp.full((wide, BLOCK), -jnp.inf, F32)
        for p in range(listed // 2):
            keys = kv_list[buf, 0, p * wide : (p + 1) * wide]
            s = lax.dot_general(q, keys, (((1,), (1,)), ((), ())), preferred_element_type=F32)
            scores[buf, :, p * wide : (p + 1) * wide] = s
            top = jnp.maximum(top, jnp.maximum(s[:, :BLOCK], s[:, BLOCK:]))
        top = jnp.max(top, axis=1, keepdims=True)
        mixed = jnp.zeros((wide, BLOCK), F32)
        for p in range(listed // 2):
            e = jnp.exp(scores[buf, :, p * wide : (p + 1) * wide] - top).astype(BF16)
            mixed += jnp.dot(e, kv_list[buf, 1, p * wide : (p + 1) * wide], preferred_element_type=F32)
        mixed = mixed / pltpu.roll(mixed, HEAD, 1)
        both = jnp.where(low, pltpu.roll(mixed[:BLOCK], HEAD, 1), mixed[BLOCK:])
        attn[t] = jnp.where(i < live[0], both, 0.0).astype(BF16)

    for n, t in enumerate((2, 1, 3, 0)):
        attend(t, n % 2)
        if t > 0:
            attn_copy(t).start()

    for d in far:
        attn_copy(d).wait_recv()
    heads = jnp.concatenate([attn[0]] + [attn_got[d - 1] for d in far], axis=1)

    def project(block):
        cols = pl.ds(pl.multiple_of(block * BLOCK, BLOCK), BLOCK)
        weight = jnp.concatenate(
            [ow[:, cols]] + [owz[pl.ds(block * 2, 2), d - 1].reshape(BLOCK, BLOCK) for d in far], axis=0
        )
        return jnp.dot(heads, weight, preferred_element_type=F32)

    for d in near:
        part[d] = project(ahead(d) * 2 + other).astype(BF16)
    part_copy.start()
    terms = [project(ahead(d) * 2 + core) for d in near]
    part_copy.wait_recv()
    for d in far:
        out_send[d - 1] = (terms[d] + part_got[d].astype(F32)).astype(BF16)
        out_copy(d).start()
    rows = pl.ds(pl.multiple_of(chip * BLOCK, BLOCK), BLOCK)
    out[rows, :] = (terms[0] + part_got[0].astype(F32)).astype(BF16)
    for d in far:
        out_got(d).wait_recv()

    part_copy.wait_send()
    for d in far:
        attn_copy(d).wait_send()
        out_copy(d).wait_send()
        o1_copy(d).wait_send()
    for e in range(1, side_y):
        o2_copy(e, True).wait_send()
    for e in range(1, side_x):
        o3_copy(e, True).wait_send()
    for j in range(CHUNKS):
        for d in near:
            mold_c_copy(j, d).wait_send()
            kv_sib(j, d).wait_send()
            kv_x(j, d).wait_send()
            for slot in range(3):
                kv_core(slot, j, d).wait_send()
        for d in far:
            mold_z_copy(j, d).wait_send()
        for t in range(3):
            kv_z_copy(j, t).wait_send()
    for d in far:
        w1_copy(d).wait_send()
        q_z_copy(d).wait_send()
        q_heads(d).wait_send()
    for e in range(1, side_x):
        w2_copy(e, True).wait_send()
    for e in range(1, side_y):
        w3_copy(e, True).wait_send()
    for d in near:
        q_core(d).wait_send()


def solution(mesh):
    regions, shards = mesh.shape["region"], mesh.shape["wshard"]
    chips = shards // 2

    def step(queries, mold, q_weight, k_weight, v_weight, o_weight, lists, live):
        rows_q, feats = queries.shape
        rows_m = mold.shape[0]
        width, kv_cols = k_weight.shape
        qblocks, listed = lists.shape
        pool_blocks = rows_m // BLOCK
        rows_j = rows_m // chips // CHUNKS
        half = rows_j // 2
        piece = half // BLOCK
        far = chips - 1
        columns = regions // 2
        dma = pltpu.SemaphoreType.DMA
        any_space = pl.BlockSpec(memory_space=pl.ANY)
        smem = pl.BlockSpec(memory_space=pltpu.SMEM)
        scratch = [
            pltpu.VMEM((rows_q, feats), BF16),
            pltpu.VMEM((shards, BLOCK, feats), BF16),
            pltpu.VMEM((chips, BLOCK, feats), BF16),
            pltpu.VMEM((far, BLOCK, feats), BF16),
            pltpu.VMEM(q_weight.shape, BF16),
            pltpu.VMEM((columns, far, width // columns, feats), BF16),
            pltpu.VMEM(k_weight.shape, BF16),
            pltpu.VMEM(v_weight.shape, BF16),
            pltpu.VMEM((width, 2 * kv_cols), BF16),
            pltpu.VMEM(o_weight.shape, BF16),
            pltpu.VMEM((rows_m, feats), BF16),
            pltpu.VMEM((CHUNKS, far, rows_j, feats), BF16),
            pltpu.VMEM((CHUNKS, chips, half, feats), BF16),
            pltpu.VMEM((CHUNKS, KV_HEADS, piece, BLOCK, 2 * HEAD), BF16),
            pltpu.VMEM((3 * pool_blocks, BLOCK, 2 * HEAD), BF16),
            pltpu.VMEM((2, 2, listed * BLOCK, 2 * HEAD), BF16),
            pltpu.VMEM((qblocks, 2 * BLOCK, 2 * HEAD), BF16),
            pltpu.VMEM((2, 2 * BLOCK, listed * BLOCK), F32),
            pltpu.SMEM((qblocks, listed), F32),
            pltpu.VMEM((columns, far, width // columns, feats), BF16),
            pltpu.VMEM((chips, BLOCK, 2 * HEAD), BF16),
            pltpu.VMEM((far, BLOCK, 2 * HEAD), BF16),
            pltpu.VMEM((chips, BLOCK, feats), BF16),
            pltpu.VMEM((chips, BLOCK, feats), BF16),
            pltpu.VMEM((far, BLOCK, feats), BF16),
            dma((6,)),
        ]
        for shape in (
            (CHUNKS, far),
            (CHUNKS, chips),
            (CHUNKS, 3),
            (3, CHUNKS, chips),
            (CHUNKS, chips),
            (CHUNKS, chips),
            (far,),
            (chips,),
            (far,),
            (far,),
            (3,),
            (regions // 8 - 1,),
            (far,),
            (regions // 8 - 1,),
            (3,),
            (far,),
            (),
            (far,),
        ):
            scratch += [dma(shape), dma(shape)]
        return pl.pallas_call(
            functools.partial(kernel, chips, regions),
            out_shape=jax.ShapeDtypeStruct((rows_q, feats), BF16),
            in_specs=[any_space] * 6 + [smem] * 2,
            out_specs=pl.BlockSpec(memory_space=pltpu.VMEM),
            scratch_shapes=scratch,
            compiler_params=pltpu.CompilerParams(
                collective_id=0, has_side_effects=True, vmem_limit_bytes=215 << 18
            ),
        )(queries, mold, q_weight, k_weight, v_weight, o_weight, lists, live)

    return jax.shard_map(
        step,
        mesh=mesh,
        in_specs=(
            P("region", "wshard"),
            P("region", "wshard"),
            P(None, "wshard"),
            P(),
            P(),
            P("wshard", None),
            P("region", None),
            P("region"),
        ),
        out_specs=P("region", "wshard"),
        check_vma=False,
    )
```

```python
import functools

import jax
import jax.numpy as jnp
from jax import lax
from jax.experimental import pallas as pl
from jax.experimental.pallas import tpu as pltpu
from jax.sharding import PartitionSpec as P

HEAD = 64
KV_HEADS = 4
BLOCK = 128
MESH = pl.DeviceIdType.MESH
CHUNKS = 2
F32, BF16 = jnp.float32, jnp.bfloat16


def kernel(
    chips,
    regions,
    queries,
    mold,
    q_weight,
    k_weight,
    v_weight,
    o_weight,
    lists,
    live,
    out,
    q_own,
    q_feats,
    q_rows,
    q_send,
    qw,
    qwz,
    kw,
    vw,
    wkv,
    ow,
    mold_own,
    mold_z,
    mold_c,
    kv_send,
    pool,
    kv_list,
    q_ext,
    scores,
    keep,
    owz,
    attn,
    attn_got,
    part,
    part_got,
    out_send,
    sem_local,
    mz_s,
    mz_r,
    mc_s,
    mc_r,
    kz_s,
    kz_r,
    kc_s,
    kc_r,
    ki_s,
    ki_r,
    kx_s,
    kx_r,
    qz_s,
    qz_r,
    qc_s,
    qc_r,
    qh_s,
    qh_r,
    w1_s,
    w1_r,
    w2_s,
    w2_r,
    w3_s,
    w3_r,
    o1_s,
    o1_r,
    o2_s,
    o2_r,
    o3_s,
    o3_r,
    az_s,
    az_r,
    pc_s,
    pc_r,
    oz_s,
    oz_r,
):
    region = lax.axis_index("region")
    shard = lax.axis_index("wshard")
    chip = shard // 2
    core = lax.rem(shard, 2)
    other = 1 - core
    odd = lax.rem(region, 2)
    qblocks, listed = lists.shape
    pool_blocks = pool.shape[0] // 3
    chip_blocks = pool_blocks // chips
    chip_rows = chip_blocks * BLOCK
    rows_j = chip_rows // CHUNKS
    half = rows_j // 2
    piece = half // BLOCK
    far = range(1, chips)
    near = range(chips)

    def ahead(d):
        return lax.rem(chip + d, chips)

    def behind(d):
        return lax.rem(chip + chips - d, chips)

    def z_peer(d):
        return (region, ahead(d) * 2 + core)

    core_peer = (region, chip * 2 + other)
    sibling = (region + 1 - 2 * odd, shard)
    x_to = (lax.rem(region + regions + 2 - 4 * odd, regions), shard)
    x_from = (lax.rem(region + regions - 2 + 4 * odd, regions), shard)
    column = region // 2
    side_x = 4
    side_y = regions // 2 // side_x
    at_x = lax.rem(column, side_x)
    at_y = column // side_x
    share = qwz.shape[2]
    step_s = 1 + 2 * odd
    offsets = (0, step_s, chips - step_s, 2)

    def x_peer(e):
        return ((at_y * side_x + lax.rem(at_x + e, side_x)) * 2 + odd, shard)

    def y_peer(e):
        return ((lax.rem(at_y + e, side_y) * side_x + at_x) * 2 + odd, shard)

    def sib_peer(d):
        return (sibling[0], ahead(d) * 2 + core)

    def remote(src, dst, send, recv, peer):
        return pltpu.make_async_remote_copy(
            src_ref=src, dst_ref=dst, send_sem=send, recv_sem=recv, device_id=peer, device_id_type=MESH
        )

    local = [
        pltpu.make_async_copy(k_weight, kw, sem_local.at[0]),
        pltpu.make_async_copy(v_weight, vw, sem_local.at[1]),
        pltpu.make_async_copy(q_weight, qw, sem_local.at[2]),
        pltpu.make_async_copy(o_weight, ow, sem_local.at[3]),
        pltpu.make_async_copy(queries, q_own, sem_local.at[4]),
        pltpu.make_async_copy(mold, mold_own, sem_local.at[5]),
    ]
    for copy in (local[5], local[2], local[3], local[0], local[1], local[4]):
        copy.start()

    barrier = pltpu.get_barrier_semaphore()
    partners = [z_peer(d) for d in far] + [core_peer, sibling, x_to, x_from]
    partners += [sib_peer(chips - step_s), sib_peer(2)]
    partners += [x_peer(e) for e in range(1, side_x)] + [y_peer(e) for e in range(1, side_y)]
    for peer in partners:
        pl.semaphore_signal(barrier, inc=1, device_id=peer, device_id_type=MESH)
    for copy in local:
        copy.wait()
    q_feats[shard] = q_own[pl.ds(pl.multiple_of(chip * BLOCK, BLOCK), BLOCK), :]
    for h in range(KV_HEADS):
        cols = slice(h * HEAD, (h + 1) * HEAD)
        wkv[:, h * 2 * HEAD : (h + 1) * 2 * HEAD] = jnp.concatenate([kw[:, cols], vw[:, cols]], axis=1)

    def mark(i, _):
        for l in range(listed):
            repeat = jnp.int32(0)
            for e in range(l):
                repeat = jnp.where(lists[i, e] == lists[i, l], jnp.int32(1), repeat)
            keep[i, l] = jnp.where(repeat == 1, F32(0.0), F32(1.0))
        return 0

    lax.fori_loop(0, qblocks, mark, 0)

    pl.semaphore_wait(barrier, len(partners))

    def w1_copy(d):
        rows = pl.ds(pl.multiple_of(column * share, share), share)
        return remote(qw.at[rows], qwz.at[column, d - 1], w1_s.at[d - 1], w1_r.at[d - 1], z_peer(d))

    def w2_copy(e, sent):
        spot = column if sent else at_y * side_x + lax.rem(at_x + side_x - e, side_x)
        return remote(qwz.at[column], qwz.at[spot], w2_s.at[e - 1], w2_r.at[e - 1], x_peer(e))

    def w3_copy(e, sent):
        mine = pl.ds(at_y * side_x, side_x)
        spot = mine if sent else pl.ds(lax.rem(at_y + side_y - e, side_y) * side_x, side_x)
        return remote(qwz.at[mine], qwz.at[spot], w3_s.at[e - 1], w3_r.at[e - 1], y_peer(e))

    column_o = at_x * side_y + at_y

    def o1_copy(d):
        rows = pl.ds(pl.multiple_of(lax.rem(column_o, 2) * share, share), share)
        cols = pl.ds(pl.multiple_of(column_o // 2 * BLOCK, BLOCK), BLOCK)
        return remote(ow.at[rows, cols], owz.at[column_o, d - 1], o1_s.at[d - 1], o1_r.at[d - 1], z_peer(d))

    def o2_copy(e, sent):
        spot = column_o if sent else at_x * side_y + lax.rem(at_y + side_y - e, side_y)
        return remote(owz.at[column_o], owz.at[spot], o2_s.at[e - 1], o2_r.at[e - 1], y_peer(e))

    def o3_copy(e, sent):
        mine = pl.ds(at_x * side_y, side_y)
        spot = mine if sent else pl.ds(lax.rem(at_x + side_x - e, side_x) * side_y, side_y)
        return remote(owz.at[mine], owz.at[spot], o3_s.at[e - 1], o3_r.at[e - 1], x_peer(e))

    for d in far:
        w1_copy(d).start()
    for d in far:
        o1_copy(d).start()

    def mold_z_copy(j, d):
        row = pl.multiple_of(ahead(d) * chip_rows + j * rows_j, BLOCK)
        return remote(
            mold_own.at[pl.ds(row, rows_j)], mold_z.at[j, d - 1], mz_s.at[j, d - 1], mz_r.at[j, d - 1], z_peer(d)
        )

    for j in range(CHUNKS):
        for d in (2, 1, 3):
            mold_z_copy(j, d).start()

    def mold_src(j, d, side):
        rows = pl.ds(pl.multiple_of(side * half, BLOCK), half)
        if d == 0:
            return mold_own.at[pl.ds(pl.multiple_of(chip * chip_rows + j * rows_j + side * half, BLOCK), half)]
        return mold_z.at[j, d - 1, rows]

    def mold_c_copy(j, d):
        return remote(mold_src(j, d, other), mold_c.at[j, d], mc_s.at[j, d], mc_r.at[j, d], core_peer)

    for j in range(CHUNKS):
        mold_c_copy(j, 0).start()

    def at_piece(slot, j, off, side):
        return pl.ds(slot * pool_blocks + behind(off) * chip_blocks + (j * 2 + side) * piece, piece)

    z_routes = ((step_s, 0), (chips - step_s, 1), (2, 1))
    z_arrivals = ((0, 1), (1, 1), (1, 3))

    def kv_z_copy(j, t):
        d, slot = z_routes[t]
        peer = sib_peer(d) if slot else z_peer(d)
        spot = at_piece(slot, j, 0, core)
        return remote(kv_send.at[j, ahead(d)], pool.at[spot], kz_s.at[j, t], kz_r.at[j, t], peer)

    def kv_z_got(j, t):
        slot, at = z_arrivals[t]
        spot = at_piece(slot, j, offsets[at], core)
        return remote(kv_send.at[j, 0], pool.at[spot], kz_s.at[j, t], kz_r.at[j, t], sibling)

    def kv_core(slot, j, t):
        spot = at_piece(slot, j, offsets[t], core)
        return remote(pool.at[spot], pool.at[spot], kc_s.at[slot, j, t], kc_r.at[slot, j, t], core_peer)

    def kv_core_got(slot, j, t):
        spot = at_piece(slot, j, offsets[t], other)
        return remote(pool.at[spot], pool.at[spot], kc_s.at[slot, j, t], kc_r.at[slot, j, t], core_peer)

    sib_sent = ((0, 0), (0, 1), (1, 1), (1, 3))
    sib_arrivals = ((1, 0), (1, 2), (0, 2), (0, 3))

    def kv_sib(j, t):
        slot, at = sib_sent[t]
        src = at_piece(slot, j, offsets[at], core)
        dst = at_piece(1 - slot, j, offsets[at], core)
        return remote(pool.at[src], pool.at[dst], ki_s.at[j, t], ki_r.at[j, t], sibling)

    def kv_sib_got(j, t):
        slot, at = sib_arrivals[t]
        spot = at_piece(slot, j, offsets[at], core)
        return remote(pool.at[spot], pool.at[spot], ki_s.at[j, t], ki_r.at[j, t], sibling)

    def kv_x(j, t):
        return remote(
            pool.at[at_piece(1, j, offsets[t], core)],
            pool.at[at_piece(2, j, offsets[t], core)],
            kx_s.at[j, t],
            kx_r.at[j, t],
            x_to,
        )

    def q_z_copy(d):
        rows = pl.ds(pl.multiple_of(ahead(d) * BLOCK, BLOCK), BLOCK)
        return remote(q_own.at[rows], q_feats.at[shard], qz_s.at[d - 1], qz_r.at[d - 1], z_peer(d))

    def q_z_got(d):
        return remote(q_send.at[0], q_feats.at[behind(d) * 2 + core], qz_s.at[d - 1], qz_r.at[d - 1], z_peer(d))

    def q_core(d):
        spot = q_feats.at[behind(d) * 2 + core]
        return remote(spot, spot, qc_s.at[d], qc_r.at[d], core_peer)

    def q_core_got(d):
        spot = q_feats.at[behind(d) * 2 + other]
        return remote(spot, spot, qc_s.at[d], qc_r.at[d], core_peer)

    def q_heads(d):
        return remote(q_send.at[d - 1], q_rows.at[chip], qh_s.at[d - 1], qh_r.at[d - 1], z_peer(d))

    def q_heads_got(d):
        return remote(q_send.at[d - 1], q_rows.at[behind(d)], qh_s.at[d - 1], qh_r.at[d - 1], z_peer(d))

    q_core(0).start()
    for d in far:
        q_z_copy(d).start()
    for d in far:
        w1_copy(d).wait_recv()
    for e in range(1, side_x):
        w2_copy(e, True).start()
    for d in far:
        o1_copy(d).wait_recv()
    for e in range(1, side_y):
        o2_copy(e, True).start()
    for e in range(1, side_x):
        w2_copy(e, False).wait_recv()
    for e in range(1, side_y):
        w3_copy(e, True).start()

    for j in range(CHUNKS):
        for d in (2, 1, 3):
            mold_z_copy(j, d).wait_recv()
            mold_c_copy(j, d).start()
        total = jnp.zeros((half, wkv.shape[1]), F32)
        for d in near:
            depth = 2 * BLOCK
            base = pl.multiple_of(behind(d) * depth, depth)
            mine = wkv[pl.ds(pl.multiple_of(base + core * BLOCK, BLOCK), BLOCK), :]
            total += jnp.dot(mold_src(j, d, core)[...], mine, preferred_element_type=F32)
            mold_c_copy(j, d).wait_recv()
            theirs = wkv[pl.ds(pl.multiple_of(base + other * BLOCK, BLOCK), BLOCK), :]
            total += jnp.dot(mold_c[j, d], theirs, preferred_element_type=F32)
        pairs = total.astype(BF16)
        for h in range(KV_HEADS):
            kv_send[j, h] = pairs[:, h * BLOCK : (h + 1) * BLOCK].reshape(piece, BLOCK, BLOCK)
        pool[at_piece(0, j, 0, core)] = kv_send[j, chip]
        for t in range(3):
            kv_z_copy(j, t).start()
        kv_sib(j, 0).start()
        kv_core(0, j, 0).start()
        if j == 0:
            for e in range(1, side_y):
                o2_copy(e, False).wait_recv()
            for e in range(1, side_x):
                o3_copy(e, True).start()

    def forward(j):
        for t in range(3):
            kv_z_got(j, t).wait_recv()
            slot, at = z_arrivals[t]
            if slot == 1:
                kv_x(j, at).start()
            kv_sib(j, t + 1).start()
            kv_core(slot, j, at).start()

    for d in far:
        q_z_got(d).wait_recv()
        q_core(d).start()
    forward(0)

    for e in range(1, side_y):
        w3_copy(e, False).wait_recv()
    for d in near:
        q_core_got(d).wait_recv()
    feats = jnp.concatenate([q_feats[f] for f in range(q_feats.shape[0])], axis=1)

    def project_q(weight):
        value = jnp.dot(feats, weight, preferred_element_type=F32).astype(BF16)
        return (value.astype(F32) * HEAD**-0.5).astype(BF16)

    for d in far:
        q_send[d - 1] = project_q(qwz[:, chips - d - 1].reshape(qw.shape))
        q_heads(d).start()
    q_rows[chip] = project_q(qw[...])

    for j in range(1, CHUNKS):
        forward(j)
    for j in range(CHUNKS):
        for t in range(4):
            kv_sib_got(j, t).wait_recv()
            slot, at = sib_arrivals[t]
            if slot == 1:
                kv_x(j, at).start()
            kv_core(slot, j, at).start()

    lane = lax.broadcasted_iota(jnp.int32, (BLOCK, 2 * HEAD), 1)
    for d in far:
        q_heads_got(d).wait_recv()
    for i in range(qblocks):
        value = q_rows[i].astype(F32)
        q_ext[i, :BLOCK] = jnp.where(lane < HEAD, value, 0.0).astype(BF16)
        q_ext[i, BLOCK:] = jnp.where(lane < HEAD, pltpu.roll(value, HEAD, 1), 0.0).astype(BF16)

    for j in range(CHUNKS):
        for t in (1, 3, 0, 2):
            kv_x(j, t).wait_recv()
            kv_core(2, j, t).start()

    for slot in range(3):
        for j in range(CHUNKS):
            for d in near:
                kv_core_got(slot, j, d).wait_recv()
    for e in range(1, side_x):
        o3_copy(e, False).wait_recv()

    low = lax.broadcasted_iota(jnp.int32, (BLOCK, 2 * HEAD), 1) < HEAD
    wide = 2 * BLOCK

    def attn_copy(t):
        return remote(attn.at[t], attn_got.at[t - 1], az_s.at[t - 1], az_r.at[t - 1], z_peer(t))

    part_copy = remote(part, part_got, pc_s, pc_r, core_peer)

    def out_copy(d):
        rows = pl.ds(pl.multiple_of(chip * BLOCK, BLOCK), BLOCK)
        return remote(out_send.at[d - 1], out.at[rows], oz_s.at[d - 1], oz_r.at[d - 1], z_peer(d))

    def out_got(d):
        rows = pl.ds(pl.multiple_of(behind(d) * BLOCK, BLOCK), BLOCK)
        return remote(out_send.at[d - 1], out.at[rows], oz_s.at[d - 1], oz_r.at[d - 1], z_peer(d))

    ones = low.astype(F32).astype(BF16)
    high = (1.0 - low.astype(F32)).astype(BF16)

    def attend(t, buf):
        i = ahead(t)
        for l in range(listed):
            block = lists[i, l]
            home = block // pool_blocks
            slot = jnp.where(home == region, 0, jnp.where(home == sibling[0], 1, 2))
            rows = slice(l * BLOCK, (l + 1) * BLOCK)
            pair = pool[slot * pool_blocks + lax.rem(block, pool_blocks)]
            kv_list[buf, 0, rows] = pair
            kv_list[buf, 1, rows] = (pair * high + ones) * jnp.full(pair.shape, keep[i, l], F32).astype(BF16)
        q = q_ext[i]
        top = jnp.full((wide, BLOCK), -jnp.inf, F32)
        for p in range(listed // 2):
            keys = kv_list[buf, 0, p * wide : (p + 1) * wide]
            s = lax.dot_general(q, keys, (((1,), (1,)), ((), ())), preferred_element_type=F32)
            scores[buf, :, p * wide : (p + 1) * wide] = s
            top = jnp.maximum(top, jnp.maximum(s[:, :BLOCK], s[:, BLOCK:]))
        top = jnp.max(top, axis=1, keepdims=True)
        mixed = jnp.zeros((wide, BLOCK), F32)
        for p in range(listed // 2):
            e = jnp.exp(scores[buf, :, p * wide : (p + 1) * wide] - top).astype(BF16)
            mixed += jnp.dot(e, kv_list[buf, 1, p * wide : (p + 1) * wide], preferred_element_type=F32)
        mixed = mixed / pltpu.roll(mixed, HEAD, 1)
        both = jnp.where(low, pltpu.roll(mixed[:BLOCK], HEAD, 1), mixed[BLOCK:])
        attn[t] = jnp.where(i < live[0], both, 0.0).astype(BF16)

    for n, t in enumerate((2, 1, 3, 0)):
        attend(t, n % 2)
        if t > 0:
            attn_copy(t).start()

    for d in far:
        attn_copy(d).wait_recv()
    heads = jnp.concatenate([attn[0]] + [attn_got[d - 1] for d in far], axis=1)

    def project(block):
        cols = pl.ds(pl.multiple_of(block * BLOCK, BLOCK), BLOCK)
        weight = jnp.concatenate(
            [ow[:, cols]] + [owz[pl.ds(block * 2, 2), d - 1].reshape(BLOCK, BLOCK) for d in far], axis=0
        )
        return jnp.dot(heads, weight, preferred_element_type=F32)

    for d in near:
        part[d] = project(ahead(d) * 2 + other).astype(BF16)
    part_copy.start()
    terms = [project(ahead(d) * 2 + core) for d in near]
    part_copy.wait_recv()
    for d in far:
        out_send[d - 1] = (terms[d] + part_got[d].astype(F32)).astype(BF16)
        out_copy(d).start()
    rows = pl.ds(pl.multiple_of(chip * BLOCK, BLOCK), BLOCK)
    out[rows, :] = (terms[0] + part_got[0].astype(F32)).astype(BF16)
    for d in far:
        out_got(d).wait_recv()

    part_copy.wait_send()
    for d in far:
        attn_copy(d).wait_send()
        out_copy(d).wait_send()
        o1_copy(d).wait_send()
    for e in range(1, side_y):
        o2_copy(e, True).wait_send()
    for e in range(1, side_x):
        o3_copy(e, True).wait_send()
    for j in range(CHUNKS):
        for d in near:
            mold_c_copy(j, d).wait_send()
            kv_sib(j, d).wait_send()
            kv_x(j, d).wait_send()
            for slot in range(3):
                kv_core(slot, j, d).wait_send()
        for d in far:
            mold_z_copy(j, d).wait_send()
        for t in range(3):
            kv_z_copy(j, t).wait_send()
    for d in far:
        w1_copy(d).wait_send()
        q_z_copy(d).wait_send()
        q_heads(d).wait_send()
    for e in range(1, side_x):
        w2_copy(e, True).wait_send()
    for e in range(1, side_y):
        w3_copy(e, True).wait_send()
    for d in near:
        q_core(d).wait_send()


def solution(mesh):
    regions, shards = mesh.shape["region"], mesh.shape["wshard"]
    chips = shards // 2

    def step(queries, mold, q_weight, k_weight, v_weight, o_weight, lists, live):
        rows_q, feats = queries.shape
        rows_m = mold.shape[0]
        width, kv_cols = k_weight.shape
        qblocks, listed = lists.shape
        pool_blocks = rows_m // BLOCK
        rows_j = rows_m // chips // CHUNKS
        half = rows_j // 2
        piece = half // BLOCK
        far = chips - 1
        columns = regions // 2
        dma = pltpu.SemaphoreType.DMA
        any_space = pl.BlockSpec(memory_space=pl.ANY)
        smem = pl.BlockSpec(memory_space=pltpu.SMEM)
        scratch = [
            pltpu.VMEM((rows_q, feats), BF16),
            pltpu.VMEM((shards, BLOCK, feats), BF16),
            pltpu.VMEM((chips, BLOCK, feats), BF16),
            pltpu.VMEM((far, BLOCK, feats), BF16),
            pltpu.VMEM(q_weight.shape, BF16),
            pltpu.VMEM((columns, far, width // columns, feats), BF16),
            pltpu.VMEM(k_weight.shape, BF16),
            pltpu.VMEM(v_weight.shape, BF16),
            pltpu.VMEM((width, 2 * kv_cols), BF16),
            pltpu.VMEM(o_weight.shape, BF16),
            pltpu.VMEM((rows_m, feats), BF16),
            pltpu.VMEM((CHUNKS, far, rows_j, feats), BF16),
            pltpu.VMEM((CHUNKS, chips, half, feats), BF16),
            pltpu.VMEM((CHUNKS, KV_HEADS, piece, BLOCK, 2 * HEAD), BF16),
            pltpu.VMEM((3 * pool_blocks, BLOCK, 2 * HEAD), BF16),
            pltpu.VMEM((2, 2, listed * BLOCK, 2 * HEAD), BF16),
            pltpu.VMEM((qblocks, 2 * BLOCK, 2 * HEAD), BF16),
            pltpu.VMEM((2, 2 * BLOCK, listed * BLOCK), F32),
            pltpu.SMEM((qblocks, listed), F32),
            pltpu.VMEM((columns, far, width // columns, feats), BF16),
            pltpu.VMEM((chips, BLOCK, 2 * HEAD), BF16),
            pltpu.VMEM((far, BLOCK, 2 * HEAD), BF16),
            pltpu.VMEM((chips, BLOCK, feats), BF16),
            pltpu.VMEM((chips, BLOCK, feats), BF16),
            pltpu.VMEM((far, BLOCK, feats), BF16),
            dma((6,)),
        ]
        for shape in (
            (CHUNKS, far),
            (CHUNKS, chips),
            (CHUNKS, 3),
            (3, CHUNKS, chips),
            (CHUNKS, chips),
            (CHUNKS, chips),
            (far,),
            (chips,),
            (far,),
            (far,),
            (3,),
            (regions // 8 - 1,),
            (far,),
            (regions // 8 - 1,),
            (3,),
            (far,),
            (),
            (far,),
        ):
            scratch += [dma(shape), dma(shape)]
        return pl.pallas_call(
            functools.partial(kernel, chips, regions),
            out_shape=jax.ShapeDtypeStruct((rows_q, feats), BF16),
            in_specs=[any_space] * 6 + [smem] * 2,
            out_specs=pl.BlockSpec(memory_space=pltpu.VMEM),
            scratch_shapes=scratch,
            compiler_params=pltpu.CompilerParams(
                collective_id=0, has_side_effects=True, vmem_limit_bytes=215 << 18
            ),
        )(queries, mold, q_weight, k_weight, v_weight, o_weight, lists, live)

    return jax.shard_map(
        step,
        mesh=mesh,
        in_specs=(
            P("region", "wshard"),
            P("region", "wshard"),
            P(None, "wshard"),
            P(),
            P(),
            P("wshard", None),
            P("region", None),
            P("region"),
        ),
        out_specs=P("region", "wshard"),
        check_vma=False,
    )
```
